1024 devices in a mesh: leaf: 128 (over x, z, core), grp: 8 (over y).
Axes of the slice: x: 4, y: 8, z: 16, core: 2. Of those that a mesh axis runs over, the one named last changes fastest.
Arguments:
- charges: bfloat16 [64, 2097152], P(None, ('leaf', 'grp')), may hold values from -6 to 6
- positions: bfloat16 [3, 2097152], P(None, ('leaf', 'grp')), may hold values from 0 to 1
- bases: bfloat16 [64, 2097152], P(None, ('leaf', 'grp')), may hold values from -0.5 to 0.5
- transfers: bfloat16 [16384, 64, 64], P(('leaf', 'grp')), may hold values from -0.1875 to 0.1875
- couplings: bfloat16 [128, 4096, 64], P('leaf', 'grp'), may hold values from -0.09375 to 0.09375
- far_source: int32 [128, 64], P('leaf'), may hold values from 0 to 127, as said below
- wanted: int32 [128, 8, 8, 8], P('leaf', 'grp'), may hold values from 0 to 15, as said below
- near_target: int32 [128, 8, 512], P('leaf', 'grp'), may hold values from 0 to 15
- near_slot: int32 [128, 8, 512], P('leaf', 'grp'), may hold values from 0 to 63, as said below
Outputs:
- potential: bfloat16 [64, 2097152], P(None, ('leaf', 'grp'))
The draws below stay inside these ranges and needn't reach their ends.
Inputs may be any that keep to these rules, and one draw needn't show every extreme that they name: `far_source`: the entries of one target's list are distinct and never the target itself. wanted[i, g, h, c] is a leaf numbered within device (i, h); the 8 entries of one [i, g, h] are distinct. `near_slot`: the value h * 8 + c names slot c of group device h.
All inputs are finite; a program needn't handle non-finite values.
Results may differ from the reference program's by a relative error of at most 0.007.
Values may be sent and summed in bfloat16 or wider, within the bound.
A program may use at most 32 MiB of HBM per device.

```python
import jax
import jax.numpy as jnp
from jax import lax

R = 64
K = 64
BS = 128
CAP = 8
DEVICE_LEAF_COUNT = 16
NEAR_DEV = 512
FAR_DEV = 8
POINTS = 2097152
N_LEAF = 128
N_GRP = 8


def slot_counts(key):
    key = jax.random.fold_in(key, 91)
    leading_key, second_key = jax.random.split(key)
    counts = jax.random.randint(leading_key, (N_LEAF, N_GRP, N_GRP), 1, CAP + 1)
    complete_sender = jax.random.randint(second_key, (N_LEAF, N_GRP, 1), 0, N_GRP)
    is_full = jnp.arange(N_GRP)[None, None, :] == complete_sender
    counts = jnp.where(is_full, CAP, counts)
    return counts.at[0, 0, N_GRP - 1].set(CAP)


def draw_near_slot(key, part):
    counts = slot_counts(key)
    key = jax.random.fold_in(key, 5)
    leading_key, second_key = jax.random.split(key)
    block_index = jnp.arange(NEAR_DEV)
    listed = (block_index < N_GRP * CAP)[None, None, :]
    sender_any = jax.random.randint(leading_key, (N_LEAF, N_GRP, NEAR_DEV), 0, N_GRP)
    sender = jnp.where(listed, (block_index // CAP % N_GRP)[None, None, :], sender_any)
    live_count = jnp.take_along_axis(counts, sender, axis=2)
    spare_slot = jax.random.randint(second_key, (N_LEAF, N_GRP, NEAR_DEV), 0, live_count)
    first_slot = (block_index % CAP)[None, None, :]
    slot_index = jnp.where(listed & (first_slot < live_count), first_slot, spare_slot)
    return (sender * CAP + slot_index).astype(jnp.int32)


def draw_wanted(key, part):
    key = jax.random.fold_in(key, 7)
    scores = jax.random.randint(key, (N_LEAF, N_GRP, N_GRP, DEVICE_LEAF_COUNT), 0, 2 ** 20) * DEVICE_LEAF_COUNT + jnp.arange(DEVICE_LEAF_COUNT)
    ordering = jnp.argsort(scores, axis=-1)
    return ordering[..., :CAP].astype(jnp.int32)


def draw_far_source(key, part):
    key = jax.random.fold_in(key, 11)
    scores = jax.random.randint(key, (N_LEAF, N_LEAF - 1), 0, 2 ** 20) * N_LEAF + jnp.arange(N_LEAF - 1)
    ordering = jnp.argsort(scores, axis=-1)[:, :N_GRP * FAR_DEV]
    return ((jnp.arange(N_LEAF)[:, None] + 1 + ordering) % N_LEAF).astype(jnp.int32)


def plant(drawn, stream_key, low, high):
    spot = [jax.random.randint(jax.random.fold_in(stream_key, axis), (), 0, length) for axis, length in enumerate(drawn.shape)]
    widest = drawn.shape.index(max(drawn.shape))
    neighbour = spot[:widest] + [(spot[widest] + 1) % drawn.shape[widest]] + spot[widest + 1:]
    return drawn.at[tuple(spot)].set(low).at[tuple(neighbour)].set(high)


def level_of(rng, shape, cuts, least, top_value):
    def one(axis_at, shards_of):
        steps = jax.random.uniform(jax.random.fold_in(jax.random.fold_in(rng, 6), axis_at), (shards_of,), jnp.float32, least / len(cuts), top_value / len(cuts))
        return jnp.repeat(jnp.exp(steps), shape[axis_at] // shards_of).reshape((-1,) + (1,) * (len(shape) - axis_at - 1))

    level = one(*cuts[0])
    for cut in cuts[1:]:
        level = level * one(*cut)
    return level


def scatter_about(stream_key, extent, width, limit, pieces=(), kind=jnp.bfloat16):
    drawn = jax.random.normal(stream_key, extent, jnp.float32) * width
    if len(pieces) > 0:
        drawn = level_of(stream_key, extent, pieces, -0.22, 0.18) * drawn
    return jnp.clip(drawn, min=-limit, max=limit).astype(kind)


def setup_inputs(seed: int = 0) -> dict:
    splits = jax.random.split(jax.random.key(seed), 10)
    return {
        "charges": scatter_about(splits[0], (R, POINTS), 1.0, 6.0, ((1, 1024),)),
        "positions": jnp.clip(1.0 * jax.random.uniform(splits[1], (3, POINTS), jnp.float32) ** level_of(splits[1], (3, POINTS), ((1, 1024),), -0.2, 0.2), 0.0, 1.0).astype(jnp.bfloat16),
        "bases": scatter_about(splits[2], (K, POINTS), BS ** -0.5, 0.5, ((1, 1024),)),
        "transfers": scatter_about(splits[3], (N_LEAF * N_GRP * DEVICE_LEAF_COUNT, K, K), (K * DEVICE_LEAF_COUNT) ** -0.5, 0.1875, ((0, 1024),)),
        "couplings": scatter_about(splits[4], (N_LEAF, N_GRP * FAR_DEV * K, K), (K * N_GRP * FAR_DEV) ** -0.5, 0.09375, ((0, 128), (1, 8))),
        "far_source": draw_far_source(jax.random.fold_in(splits[9], 71), 0),
        "wanted": draw_wanted(jax.random.fold_in(splits[9], 71), 0),
        "near_target": plant(jax.random.randint(splits[7], (N_LEAF, N_GRP, NEAR_DEV), 0, DEVICE_LEAF_COUNT), jax.random.fold_in(splits[7], 1), 0, DEVICE_LEAF_COUNT - 1).astype(jnp.int32),
        "near_slot": draw_near_slot(jax.random.fold_in(splits[9], 71), 0),
    }


soften = 0.05

def kernel_block(target_pos, source_pos, leaf_size):
    offset = target_pos[:, :, :, None] - source_pos[:, :, None, :]
    squared = lax.optimization_barrier(jnp.sum(offset * offset, axis=0))
    return (1.0 / (leaf_size * jnp.sqrt(squared + soften * soften))).astype(jnp.bfloat16)

def reference(charges, positions, bases, transfers, couplings, far_source, wanted, near_target, near_slot):
    group_leaves = N_GRP * DEVICE_LEAF_COUNT
    charge_all = charges.reshape(R, N_LEAF, group_leaves, BS)
    pos_all = positions.reshape(3, N_LEAF, group_leaves, BS)
    basis_all = bases.reshape(K, N_LEAF, group_leaves, BS)
    transfer_all = transfers.reshape(N_LEAF, group_leaves, K, K)

    def upward(cluster):
        charge_group = lax.dynamic_index_in_dim(charge_all, cluster, 1, False).astype(jnp.float32)
        basis_group = lax.dynamic_index_in_dim(basis_all, cluster, 1, False).astype(jnp.float32)
        transfer_group = transfer_all[cluster].astype(jnp.float32)
        leaf_coeff = jnp.einsum('kln,rln->lkr', basis_group, charge_group).astype(jnp.bfloat16)
        return jnp.einsum('lab,lbr->ar', transfer_group, leaf_coeff.astype(jnp.float32)).astype(jnp.bfloat16)
    cluster_coeff = lax.map(upward, jnp.arange(N_LEAF, dtype=jnp.int32))
    surface_panels = couplings.reshape(N_LEAF, N_GRP * FAR_DEV, K, K).astype(jnp.float32)
    selected_entries = cluster_coeff[far_source].astype(jnp.float32)
    target_coefficient = jnp.einsum('lksm,lkmw->lsw', surface_panels, selected_entries).astype(jnp.bfloat16)
    member = jnp.arange(N_GRP, dtype=jnp.int32)[None, :, None]
    receiving_leaf = near_target + member * DEVICE_LEAF_COUNT
    sender = near_slot // CAP
    flat_wanted = wanted.reshape(N_LEAF, N_GRP, N_GRP * CAP)
    source_leaf = jnp.take_along_axis(flat_wanted, near_slot, axis=2) + sender * DEVICE_LEAF_COUNT
    block_count = N_GRP * NEAR_DEV
    target_lists = receiving_leaf.reshape(N_LEAF, block_count // 16, 16)
    source_lists = source_leaf.reshape(N_LEAF, block_count // 16, 16)

    def downward(cluster):
        charge_group = lax.dynamic_index_in_dim(charge_all, cluster, 1, False).astype(jnp.float32)
        pos_group = lax.dynamic_index_in_dim(pos_all, cluster, 1, False).astype(jnp.float32)
        basis_group = lax.dynamic_index_in_dim(basis_all, cluster, 1, False).astype(jnp.float32)
        transfer_group = transfer_all[cluster].astype(jnp.float32)
        leaf_of_target = jnp.einsum('lab,ar->lbr', transfer_group, target_coefficient[cluster].astype(jnp.float32)).astype(jnp.bfloat16)
        far_part = jnp.einsum('kln,lkr->rln', basis_group, leaf_of_target.astype(jnp.float32))

        def add_batch(total, lists):
            target_ids, source_ids = lists
            block = kernel_block(jnp.take(pos_group, target_ids, axis=1), jnp.take(pos_group, source_ids, axis=1), BS)
            source_rows = jnp.take(charge_group, source_ids, axis=1)
            contribution = jnp.einsum('rjb,jab->rja', source_rows, block.astype(jnp.float32))
            return (total.at[:, target_ids, :].add(contribution), None)
        start = jnp.zeros((R, group_leaves, BS), jnp.float32)
        near_part, _ = lax.scan(add_batch, start, (target_lists[cluster], source_lists[cluster]))
        return (near_part + far_part).astype(jnp.bfloat16)
    potential = lax.map(downward, jnp.arange(N_LEAF, dtype=jnp.int32))
    return jnp.transpose(potential, (1, 0, 2, 3)).reshape(R, N_LEAF * group_leaves * BS)
```

```python
import functools

import jax
import jax.numpy as jnp
from jax import lax
from jax.experimental import pallas as pl
from jax.experimental.pallas import tpu as pltpu
from jax.sharding import PartitionSpec as P

MESH = pl.DeviceIdType.MESH
bf = jnp.bfloat16
f32 = jnp.float32
GRP = 8
LEAVES = 16
BS = 128
CAP = 8
HALF = LEAVES // 2
FEATS = 16
SOFTEN2 = 0.05 * 0.05
SCALE = float(BS * BS)
NT = (((1,), (1,)), ((), ()))


def dot_nt(a, b):
    return lax.dot_general(a, b, NT, preferred_element_type=f32)


def dot(a, b):
    return jnp.dot(a, b, preferred_element_type=f32)


def pack(x):
    return jnp.concatenate([x[:32, :], x[32:, :]], axis=1)


def unpack(x):
    return jnp.concatenate([x[:, :64], x[:, 64:]], axis=0)


def pieces(n):
    high = n.astype(bf).astype(f32)
    rest = n - high
    middle = rest.astype(bf).astype(f32)
    return high, middle, rest - middle


def kernel(
    dims,
    wanted,
    far_source,
    charges,
    positions,
    bases,
    transfers,
    couplings,
    near_target,
    near_slot,
    out,
    ch0,
    ch1,
    ch2,
    ch3,
    ch4,
    ch5,
    ch6,
    ch7,
    ps0,
    ps1,
    ps2,
    ps3,
    ps4,
    ps5,
    ps6,
    ps7,
    pos_rows,
    target_feat,
    source_feat,
    feat_sel,
    feat_sel_t,
    charge_sel,
    weight,
    acc,
    part_up,
    part_down,
    coeffs,
    ring_send,
    ring_recv,
    pos_send,
    pos_recv,
    up_send,
    up_recv,
    down_send,
    down_recv,
    z_send,
    z_recv,
    x_send,
    x_recv,
    core_send,
    core_recv,
):
    X, Z, C = dims
    leaf = lax.axis_index("leaf")
    y = lax.axis_index("grp")
    x = leaf // (Z * C)
    z = (leaf // C) % Z
    core = leaf % C
    chunk = [ch0, ch1, ch2, ch3, ch4, ch5, ch6, ch7]
    place = [ps0, ps1, ps2, ps3, ps4, ps5, ps6, ps7]

    def y_peer(k):
        return (leaf, (y + k) % GRP)

    def z_peer(k):
        return ((x * Z + (z + k) % Z) * C + core, y)

    def x_peer(k):
        return ((((x + k) % X) * Z + z) * C + core, y)

    core_peer = ((x * Z + z) * C + (1 - core), y)

    barrier = pltpu.get_barrier_semaphore()

    def greet(peer):
        pl.semaphore_signal(barrier, inc=1, device_id=peer, device_id_type=MESH)

    for k in range(1, GRP):
        greet(y_peer(k))
    for k in range(1, Z):
        greet(z_peer(k))
    for k in range(1, X):
        greet(x_peer(k))
    if C > 1:
        greet(core_peer)

    pos = positions[...].astype(f32)
    for d in range(3):
        for t in range(LEAVES):
            row = d * LEAVES + t
            pos_rows[row : row + 1, :] = pos[d : d + 1, t * BS : (t + 1) * BS]
    ps0[...] = pos_rows[...].astype(bf)
    for t in range(LEAVES):
        ch0[t] = charges[:, t * BS : (t + 1) * BS]

    partial = None
    for t in range(LEAVES):
        cols = slice(t * BS, (t + 1) * BS)
        leaf_coeff = dot_nt(charges[:, cols], bases[:, cols]).astype(bf)
        term = dot_nt(leaf_coeff, transfers[t])
        partial = term if partial is None else partial + term
    part_up[0] = pack(partial).astype(bf)

    pl.semaphore_wait(barrier, (GRP - 1) + (Z - 1) + (X - 1) + (C - 1))

    def exchange(buf, send, recv, k):
        return pltpu.make_async_remote_copy(
            src_ref=buf.at[0],
            dst_ref=buf.at[k],
            send_sem=send.at[k],
            recv_sem=recv.at[k],
            device_id=y_peer(k),
            device_id_type=MESH,
        )

    def ring(right, step, half):
        src = step if right else (GRP - step) % GRP
        dst = step + 1 if right else GRP - step - 1
        part = pl.ds(half * HALF, HALF)
        way = 0 if right else 1
        slot = 2 * step + (half if step < 3 else 0)
        return pltpu.make_async_remote_copy(
            src_ref=chunk[src].at[part],
            dst_ref=chunk[dst].at[part],
            send_sem=ring_send.at[way, slot],
            recv_sem=ring_recv.at[way, slot],
            device_id=y_peer(1 if right else GRP - 1),
            device_id_type=MESH,
        )

    def ring_pos(right, step):
        src = step if right else (GRP - step) % GRP
        dst = step + 1 if right else GRP - step - 1
        way = 0 if right else 1
        return pltpu.make_async_remote_copy(
            src_ref=place[src],
            dst_ref=place[dst],
            send_sem=pos_send.at[way, step],
            recv_sem=pos_recv.at[way, step],
            device_id=y_peer(1 if right else GRP - 1),
            device_id_type=MESH,
        )

    def slot_of(x_at, z_at):
        return (core * X + x_at) * Z + z_at

    def z_copy(k, z_at):
        here = coeffs.at[slot_of(x, z_at)]
        return pltpu.make_async_remote_copy(
            src_ref=here,
            dst_ref=here,
            send_sem=z_send.at[k],
            recv_sem=z_recv.at[k],
            device_id=z_peer(k),
            device_id_type=MESH,
        )

    def x_copy(k, x_at):
        here = coeffs.at[pl.ds(slot_of(x_at, 0), Z)]
        return pltpu.make_async_remote_copy(
            src_ref=here,
            dst_ref=here,
            send_sem=x_send.at[k],
            recv_sem=x_recv.at[k],
            device_id=x_peer(k),
            device_id_type=MESH,
        )

    def core_copy(core_at):
        here = coeffs.at[pl.ds(core_at * (X * Z), X * Z)]
        return pltpu.make_async_remote_copy(
            src_ref=here,
            dst_ref=here,
            send_sem=core_send,
            recv_sem=core_recv,
            device_id=core_peer,
            device_id_type=MESH,
        )

    for k in range(1, GRP):
        exchange(part_up, up_send, up_recv, k).start()
    for right in (True, False):
        ring_pos(right, 0).start()
    for half in (0, 1):
        for right in (True, False):
            ring(right, 0, half).start()

    norm = jnp.sum(pos * pos, axis=0, keepdims=True) + SOFTEN2
    high, middle, low = pieces(norm)
    one = jnp.ones_like(norm)
    target_feat[...] = (
        jnp.concatenate(
            [-2.0 * pos, high, middle, low, one, one, one, jnp.zeros((FEATS - 9, norm.shape[1]), f32)],
            axis=0,
        )
        * SCALE
    ).astype(bf)
    source_feat[...] = jnp.zeros_like(source_feat)
    for f in (3, 4, 5):
        source_feat[:, f, :] = jnp.ones((LEAVES, BS), f32)

    blocks = near_slot.shape[1]
    slot_hot = (
        lax.broadcasted_iota(jnp.int32, (GRP * CAP, blocks), 0) == near_slot[...]
    ).astype(f32)
    leaf_hot = (
        lax.broadcasted_iota(jnp.int32, (LEAVES, blocks), 0) == near_target[...]
    ).astype(f32)
    counts = dot_nt(slot_hot.astype(bf), leaf_hot.astype(bf))
    spread = (
        lax.broadcasted_iota(jnp.int32, (LEAVES, LEAVES * BS), 1) // BS
        == lax.broadcasted_iota(jnp.int32, (LEAVES, LEAVES * BS), 0)
    ).astype(f32)
    spread_counts = dot(counts.astype(bf), spread.astype(bf))
    for h in range(GRP):
        weight[h] = spread_counts[h * CAP : (h + 1) * CAP, :]

    def near(rel, first=False, last=False):
        h = (y + (GRP - rel)) % GRP
        rows = place[rel][...].astype(f32)
        px, py, pz = rows[0:16], rows[16:32], rows[32:48]
        parts = pieces(px * px + py * py + pz * pz)
        for f, v in zip((0, 1, 2, 6, 7, 8), (px, py, pz) + parts):
            source_feat[:, f, :] = v
        for c in range(CAP):
            at = wanted[h, c]
            cols = slice(c * BS, (c + 1) * BS)
            charge_sel[:, cols] = chunk[rel][at]
            feat_sel[:, cols] = source_feat[at]
        feat_sel_t[...] = feat_sel[...].T.astype(bf)
        width, depth = 1024, 512

        def block(i, carry):
            cols = pl.ds(pl.multiple_of(i * width, width), width)
            targets = target_feat[:, cols]
            w = weight[h, :, cols].astype(bf)
            total = None
            for k in range(0, CAP * BS, depth):
                dist = dot(feat_sel_t[k : k + depth, :], targets)
                g = lax.rsqrt(dist.astype(bf))
                g = jnp.concatenate(
                    [
                        g[j * BS : (j + 1) * BS, :] * w[k // BS + j : k // BS + j + 1, :]
                        for j in range(depth // BS)
                    ],
                    axis=0,
                )
                term = dot(charge_sel[:, k : k + depth], g)
                total = term if total is None else total + term
            if not first:
                total = total + acc[:, cols]
            if last:
                out[:, cols] = total.astype(bf)
            else:
                acc[:, cols] = total
            return carry

        lax.fori_loop(0, LEAVES * BS // width, block, 0)

    def arrived(step, half, right=True, left=True):
        for way in (True, False):
            if (right if way else left):
                if half == 0 or step == 3:
                    if not (step == 3 and not way):
                        ring_pos(way, step).wait_recv()
                        if step < 2 or (step == 2 and way):
                            ring_pos(way, step + 1).start()
                ring(way, step, half).wait_recv()
                if step < 2:
                    ring(way, step + 1, half).start()
                elif step == 2 and (half == 0) == way:
                    ring(way, 3, half).start()

    near(0, first=True)
    arrived(0, 0)

    for k in range(1, GRP):
        exchange(part_up, up_send, up_recv, k).wait_recv()
    total = part_up[0].astype(f32)
    for k in range(1, GRP):
        total = total + part_up[k].astype(f32)
    coeffs[slot_of(x, z)] = total.astype(bf)
    for k in range(1, Z):
        z_copy(k, z).start()

    arrived(0, 1)
    near(1)
    for k in range(1, Z):
        z_copy(k, (z + (Z - k)) % Z).wait_recv()
    for k in range(1, X):
        x_copy(k, x).start()
    arrived(1, 0)
    near(7)
    for k in range(1, X):
        x_copy(k, (x + (X - k)) % X).wait_recv()
    if C > 1:
        core_copy(core).start()
    arrived(1, 1)
    near(2)
    arrived(2, 0)
    near(6)
    if C > 1:
        core_copy(1 - core).wait_recv()

    partial = None
    rank = couplings.shape[1]
    for j in range(couplings.shape[0] // rank):
        source = far_source[0, y * (couplings.shape[0] // rank) + j]
        slot = source if C == 1 else (source & 1) * (X * Z) + (source >> 1)
        term = dot_nt(unpack(coeffs[slot]), couplings[j * rank : (j + 1) * rank, :])
        partial = term if partial is None else partial + term
    part_down[0] = pack(partial).astype(bf)
    for k in range(1, GRP):
        exchange(part_down, down_send, down_recv, k).start()

    arrived(2, 1)
    near(3)

    for k in range(1, GRP):
        exchange(part_down, down_send, down_recv, k).wait_recv()
    total = part_down[0].astype(f32)
    for k in range(1, GRP):
        total = total + part_down[k].astype(f32)
    target_coeff = unpack(total.astype(bf))
    for t in range(LEAVES):
        cols = slice(t * BS, (t + 1) * BS)
        leaf_target = dot(target_coeff, transfers[t]).astype(bf)
        acc[:, cols] += dot(leaf_target, bases[:, cols])

    near(5)
    arrived(3, 0, left=False)
    arrived(3, 1, right=False)
    near(4, last=True)

    for k in range(1, GRP):
        exchange(part_up, up_send, up_recv, k).wait_send()
        exchange(part_down, down_send, down_recv, k).wait_send()
    for right in (True, False):
        for step in range(3):
            ring_pos(right, step).wait_send()
            for half in (0, 1):
                ring(right, step, half).wait_send()
    ring_pos(True, 3).wait_send()
    ring(True, 3, 0).wait_send()
    ring(False, 3, 1).wait_send()
    for k in range(1, Z):
        z_copy(k, z).wait_send()
    for k in range(1, X):
        x_copy(k, x).wait_send()
    if C > 1:
        core_copy(core).wait_send()


def solution(mesh):
    n_leaf = mesh.shape["leaf"]
    dims = {128: (4, 16, 2), 1: (1, 1, 1), 2: (1, 1, 2), 8: (2, 2, 2), 16: (2, 4, 2)}[n_leaf]
    X, Z, C = dims

    def shards(charges, positions, bases, transfers, couplings, far_source, wanted, near_target, near_slot):
        vmem = pl.BlockSpec(memory_space=pltpu.VMEM)
        smem = pl.BlockSpec(memory_space=pltpu.SMEM)
        rows, points = charges.shape
        dma = pltpu.SemaphoreType.DMA
        return pl.pallas_call(
            functools.partial(kernel, dims),
            out_shape=jax.ShapeDtypeStruct(charges.shape, bf),
            in_specs=[smem, smem] + [vmem] * 7,
            out_specs=vmem,
            scratch_shapes=[pltpu.VMEM((LEAVES, rows, BS), bf)] * 8
            + [pltpu.VMEM((3 * LEAVES, BS), bf)] * 8
            + [
                pltpu.VMEM((3 * LEAVES, BS), f32),
                pltpu.VMEM((FEATS, points), bf),
                pltpu.VMEM((LEAVES, FEATS, BS), f32),
                pltpu.VMEM((FEATS, CAP * BS), f32),
                pltpu.VMEM((CAP * BS, FEATS), bf),
                pltpu.VMEM((rows, CAP * BS), bf),
                pltpu.VMEM((GRP, CAP, points), f32),
                pltpu.VMEM((rows, points), f32),
                pltpu.VMEM((GRP, 32, 128), bf),
                pltpu.VMEM((GRP, 32, 128), bf),
                pltpu.VMEM((X * Z * C, 32, 128), bf),
                dma((2, 7)),
                dma((2, 7)),
                dma((2, 4)),
                dma((2, 4)),
                dma((GRP,)),
                dma((GRP,)),
                dma((GRP,)),
                dma((GRP,)),
                dma((Z,)),
                dma((Z,)),
                dma((X,)),
                dma((X,)),
                dma,
                dma,
            ],
            compiler_params=pltpu.CompilerParams(
                collective_id=0, has_side_effects=True, vmem_limit_bytes=40 << 20
            ),
        )(
            wanted[0, 0],
            far_source,
            charges,
            positions,
            bases,
            transfers,
            couplings[0],
            near_target[0],
            near_slot[0],
        )

    in_specs = (
        P(None, ("leaf", "grp")),
        P(None, ("leaf", "grp")),
        P(None, ("leaf", "grp")),
        P(("leaf", "grp"), None, None),
        P("leaf", "grp", None),
        P("leaf", None),
        P("leaf", "grp", None, None),
        P("leaf", "grp", None),
        P("leaf", "grp", None),
    )
    out_specs = P(None, ("leaf", "grp"))
    return jax.shard_map(shards, mesh=mesh, in_specs=in_specs, out_specs=out_specs, check_vma=False)
```

```python
import functools

import jax
import jax.numpy as jnp
from jax import lax
from jax.experimental import pallas as pl
from jax.experimental.pallas import tpu as pltpu
from jax.sharding import PartitionSpec as P

MESH = pl.DeviceIdType.MESH
bf = jnp.bfloat16
f32 = jnp.float32
GRP = 8
LEAVES = 16
BS = 128
CAP = 8
HALF = LEAVES // 2
FEATS = 16
SOFTEN2 = 0.05 * 0.05
SCALE = float(BS * BS)
NT = (((1,), (1,)), ((), ()))


def dot_nt(a, b):
    return lax.dot_general(a, b, NT, preferred_element_type=f32)


def dot(a, b):
    return jnp.dot(a, b, preferred_element_type=f32)


def pack(x):
    return jnp.concatenate([x[:32, :], x[32:, :]], axis=1)


def unpack(x):
    return jnp.concatenate([x[:, :64], x[:, 64:]], axis=0)


def pieces(n):
    high = n.astype(bf).astype(f32)
    rest = n - high
    middle = rest.astype(bf).astype(f32)
    return high, middle, rest - middle


def kernel(
    dims,
    wanted_in,
    far_source_in,
    charges_in,
    positions_in,
    bases_in,
    transfers_in,
    couplings_in,
    near_target_in,
    near_slot_in,
    out,
    wanted,
    far_source,
    charges,
    positions,
    bases,
    transfers,
    couplings,
    near_target,
    near_slot,
    in_sem,
    ch0,
    ch1,
    ch2,
    ch3,
    ch4,
    ch5,
    ch6,
    ch7,
    ps0,
    ps1,
    ps2,
    ps3,
    ps4,
    ps5,
    ps6,
    ps7,
    pos_rows,
    target_feat,
    source_feat,
    feat_sel,
    feat_sel_t,
    charge_sel,
    weight,
    acc,
    part_up,
    part_down,
    coeffs,
    ring_send,
    ring_recv,
    pos_send,
    pos_recv,
    up_send,
    up_recv,
    down_send,
    down_recv,
    z_send,
    z_recv,
    x_send,
    x_recv,
    core_send,
    core_recv,
    ready,
):
    X, Z, C = dims
    leaf = lax.axis_index("leaf")
    y = lax.axis_index("grp")
    x = leaf // (Z * C)
    z = (leaf // C) % Z
    core = leaf % C
    chunk = [ch0, ch1, ch2, ch3, ch4, ch5, ch6, ch7]
    place = [ps0, ps1, ps2, ps3, ps4, ps5, ps6, ps7]

    def y_peer(k):
        return (leaf, (y + k) % GRP)

    def z_peer(k):
        return ((x * Z + (z + k) % Z) * C + core, y)

    def x_peer(k):
        return ((((x + k) % X) * Z + z) * C + core, y)

    core_peer = ((x * Z + z) * C + (1 - core), y)

    ins = [
        (charges_in, charges),
        (positions_in, positions),
        (bases_in, bases),
        (transfers_in, transfers),
        (near_target_in, near_target),
        (near_slot_in, near_slot),
        (wanted_in, wanted),
        (far_source_in, far_source),
        (couplings_in, couplings),
    ]

    def fetch(i):
        return pltpu.make_async_copy(ins[i][0], ins[i][1], in_sem.at[i])

    for i in range(len(ins)):
        fetch(i).start()

    barrier = pltpu.get_barrier_semaphore()

    def greet(peer):
        pl.semaphore_signal(barrier, inc=1, device_id=peer, device_id_type=MESH)

    for k in range(1, GRP):
        greet(y_peer(k))
    for k in range(1, X):
        greet(x_peer(k))
    if C > 1:
        greet(core_peer)
    for k in range(1, Z):

        @pl.when(z + k < Z)
        def _():
            greet(z_peer(k))

    for i in range(4):
        fetch(i).wait()

    pos = positions[...].astype(f32)
    for d in range(3):
        for t in range(LEAVES):
            row = d * LEAVES + t
            pos_rows[row : row + 1, :] = pos[d : d + 1, t * BS : (t + 1) * BS]
    ps0[...] = pos_rows[...].astype(bf)
    for t in range(LEAVES):
        ch0[t] = charges[:, t * BS : (t + 1) * BS]

    partial = None
    for t in range(LEAVES):
        cols = slice(t * BS, (t + 1) * BS)
        leaf_coeff = dot_nt(charges[:, cols], bases[:, cols]).astype(bf)
        term = dot_nt(leaf_coeff, transfers[t])
        partial = term if partial is None else partial + term
    part_up[0] = pack(partial).astype(bf)

    pl.semaphore_wait(barrier, (GRP - 1) + (X - 1) + (C - 1) + z)
    for k in range(1, Z):

        @pl.when(k <= z)
        def _():
            pl.semaphore_signal(ready, inc=1, device_id=z_peer(Z - k), device_id_type=MESH)


    def exchange(buf, send, recv, k):
        return pltpu.make_async_remote_copy(
            src_ref=buf.at[0],
            dst_ref=buf.at[k],
            send_sem=send.at[k],
            recv_sem=recv.at[k],
            device_id=y_peer(k),
            device_id_type=MESH,
        )

    def ring(right, step, half):
        src = step if right else (GRP - step) % GRP
        dst = step + 1 if right else GRP - step - 1
        part = pl.ds(half * HALF, HALF)
        way = 0 if right else 1
        slot = 2 * step + (half if step < 3 else 0)
        return pltpu.make_async_remote_copy(
            src_ref=chunk[src].at[part],
            dst_ref=chunk[dst].at[part],
            send_sem=ring_send.at[way, slot],
            recv_sem=ring_recv.at[way, slot],
            device_id=y_peer(1 if right else GRP - 1),
            device_id_type=MESH,
        )

    def ring_pos(right, step):
        src = step if right else (GRP - step) % GRP
        dst = step + 1 if right else GRP - step - 1
        way = 0 if right else 1
        return pltpu.make_async_remote_copy(
            src_ref=place[src],
            dst_ref=place[dst],
            send_sem=pos_send.at[way, step],
            recv_sem=pos_recv.at[way, step],
            device_id=y_peer(1 if right else GRP - 1),
            device_id_type=MESH,
        )

    def slot_of(x_at, z_at):
        return (core * X + x_at) * Z + z_at

    def z_copy(up, k, z_at):
        here = coeffs.at[slot_of(x, z_at)]
        return pltpu.make_async_remote_copy(
            src_ref=here,
            dst_ref=here,
            send_sem=z_send.at[up, k],
            recv_sem=z_recv.at[up, k],
            device_id=z_peer(k if up else Z - k),
            device_id_type=MESH,
        )

    def each_z(up, do):
        for k in range(1, Z):

            @pl.when(z + k < Z if up else k <= z)
            def _():
                do(k)

    def x_copy(k, x_at):
        here = coeffs.at[pl.ds(slot_of(x_at, 0), Z)]
        return pltpu.make_async_remote_copy(
            src_ref=here,
            dst_ref=here,
            send_sem=x_send.at[k],
            recv_sem=x_recv.at[k],
            device_id=x_peer(k),
            device_id_type=MESH,
        )

    def core_copy(core_at):
        here = coeffs.at[pl.ds(core_at * (X * Z), X * Z)]
        return pltpu.make_async_remote_copy(
            src_ref=here,
            dst_ref=here,
            send_sem=core_send,
            recv_sem=core_recv,
            device_id=core_peer,
            device_id_type=MESH,
        )

    for k in range(1, GRP):
        exchange(part_up, up_send, up_recv, k).start()
    for right in (True, False):
        ring_pos(right, 0).start()
    for half in (0, 1):
        for right in (True, False):
            ring(right, 0, half).start()

    norm = jnp.sum(pos * pos, axis=0, keepdims=True) + SOFTEN2
    high, middle, low = pieces(norm)
    one = jnp.ones_like(norm)
    target_feat[...] = (
        jnp.concatenate(
            [-2.0 * pos, high, middle, low, one, one, one, jnp.zeros((FEATS - 9, norm.shape[1]), f32)],
            axis=0,
        )
        * SCALE
    ).astype(bf)
    source_feat[...] = jnp.zeros_like(source_feat)
    for f in (3, 4, 5):
        source_feat[:, f, :] = jnp.ones((LEAVES, BS), f32)

    for i in range(4, 8):
        fetch(i).wait()

    blocks = near_slot.shape[1]
    slot_hot = (
        lax.broadcasted_iota(jnp.int32, (GRP * CAP, blocks), 0) == near_slot[...]
    ).astype(f32)
    leaf_hot = (
        lax.broadcasted_iota(jnp.int32, (LEAVES, blocks), 0) == near_target[...]
    ).astype(f32)
    counts = dot_nt(slot_hot.astype(bf), leaf_hot.astype(bf))
    spread = (
        lax.broadcasted_iota(jnp.int32, (LEAVES, LEAVES * BS), 1) // BS
        == lax.broadcasted_iota(jnp.int32, (LEAVES, LEAVES * BS), 0)
    ).astype(f32)
    spread_counts = dot(counts.astype(bf), spread.astype(bf))
    for h in range(GRP):
        weight[h] = spread_counts[h * CAP : (h + 1) * CAP, :]

    def near(rel, first=False):
        h = (y + (GRP - rel)) % GRP
        rows = place[rel][...].astype(f32)
        px, py, pz = rows[0:16], rows[16:32], rows[32:48]
        parts = pieces(px * px + py * py + pz * pz)
        for f, v in zip((0, 1, 2, 6, 7, 8), (px, py, pz) + parts):
            source_feat[:, f, :] = v
        for c in range(CAP):
            at = wanted[h, c]
            cols = slice(c * BS, (c + 1) * BS)
            charge_sel[:, cols] = chunk[rel][at]
            feat_sel[:, cols] = source_feat[at]
        feat_sel_t[...] = feat_sel[...].T.astype(bf)
        width, depth = 1024, 512

        def block(i, carry):
            cols = pl.ds(pl.multiple_of(i * width, width), width)
            targets = target_feat[:, cols]
            w = weight[h, :, cols].astype(bf)
            total = None
            for k in range(0, CAP * BS, depth):
                dist = dot(feat_sel_t[k : k + depth, :], targets)
                g = lax.rsqrt(dist.astype(bf))
                g = jnp.concatenate(
                    [
                        g[j * BS : (j + 1) * BS, :] * w[k // BS + j : k // BS + j + 1, :]
                        for j in range(depth // BS)
                    ],
                    axis=0,
                )
                term = dot(charge_sel[:, k : k + depth], g)
                total = term if total is None else total + term
            if not first:
                total = total + acc[:, cols]
            acc[:, cols] = total
            return carry

        lax.fori_loop(0, LEAVES * BS // width, block, 0)

    def arrived(step, half, right=True, left=True):
        for way in (True, False):
            if (right if way else left):
                if half == 0 or step == 3:
                    if not (step == 3 and not way):
                        ring_pos(way, step).wait_recv()
                        if step < 2 or (step == 2 and way):
                            ring_pos(way, step + 1).start()
                ring(way, step, half).wait_recv()
                if step < 2:
                    ring(way, step + 1, half).start()
                elif step == 2 and (half == 0) == way:
                    ring(way, 3, half).start()

    near(0, first=True)
    arrived(0, 0)

    for k in range(1, GRP):
        exchange(part_up, up_send, up_recv, k).wait_recv()
    total = part_up[0].astype(f32)
    for k in range(1, GRP):
        total = total + part_up[k].astype(f32)
    coeffs[slot_of(x, z)] = total.astype(bf)
    each_z(0, lambda k: z_copy(0, k, z).start())

    arrived(0, 1)
    near(1)
    arrived(1, 0)
    near(7)
    arrived(1, 1)
    near(2)
    arrived(2, 0)
    near(6)
    arrived(2, 1)

    @pl.when(z < Z - 1)
    def _():
        pl.semaphore_wait(ready, Z - 1 - z)

    each_z(1, lambda k: z_copy(1, k, z).start())
    each_z(1, lambda k: z_copy(0, k, z + k).wait_recv())
    each_z(0, lambda k: z_copy(1, k, z - k).wait_recv())
    for k in range(1, X):
        x_copy(k, x).start()
    near(3)
    for k in range(1, X):
        x_copy(k, (x + (X - k)) % X).wait_recv()
    if C > 1:
        core_copy(core).start()
    near(5)
    if C > 1:
        core_copy(1 - core).wait_recv()

    rank = couplings.shape[0]
    count = couplings.shape[1] // rank
    fetch(8).wait()
    sums = [None, None]
    for j in range(count):
        source = far_source[0, y * count + j]
        slot = source if C == 1 else (source & 1) * (X * Z) + (source >> 1)
        pair = couplings[:, j // 2 * 2 * rank : (j // 2 + 1) * 2 * rank]
        term = dot(unpack(coeffs[slot]), pair)
        sums[j % 2] = term if sums[j % 2] is None else sums[j % 2] + term
    part_down[0] = pack(sums[0][:, :rank] + sums[1][:, rank:]).astype(bf)
    for k in range(1, GRP):
        exchange(part_down, down_send, down_recv, k).start()

    arrived(3, 0, left=False)
    arrived(3, 1, right=False)
    near(4)

    for k in range(1, GRP):
        exchange(part_down, down_send, down_recv, k).wait_recv()
    total = part_down[0].astype(f32)
    for k in range(1, GRP):
        total = total + part_down[k].astype(f32)
    target_coeff = unpack(total.astype(bf))
    for t in range(LEAVES):
        cols = slice(t * BS, (t + 1) * BS)
        leaf_target = dot(target_coeff, transfers[t]).astype(bf)
        out[:, cols] = (acc[:, cols] + dot(leaf_target, bases[:, cols])).astype(bf)

    for k in range(1, GRP):
        exchange(part_up, up_send, up_recv, k).wait_send()
        exchange(part_down, down_send, down_recv, k).wait_send()
    for right in (True, False):
        for step in range(3):
            ring_pos(right, step).wait_send()
            for half in (0, 1):
                ring(right, step, half).wait_send()
    ring_pos(True, 3).wait_send()
    ring(True, 3, 0).wait_send()
    ring(False, 3, 1).wait_send()
    for up in (0, 1):
        each_z(up, lambda k: z_copy(up, k, z).wait_send())
    for k in range(1, X):
        x_copy(k, x).wait_send()
    if C > 1:
        core_copy(core).wait_send()


def solution(mesh):
    n_leaf = mesh.shape["leaf"]
    dims = {128: (4, 16, 2), 1: (1, 1, 1), 2: (1, 1, 2), 8: (2, 2, 2), 16: (2, 4, 2)}[n_leaf]
    X, Z, C = dims

    def shards(charges, positions, bases, transfers, couplings, far_source, wanted, near_target, near_slot):
        vmem = pl.BlockSpec(memory_space=pltpu.VMEM)
        hbm = pl.BlockSpec(memory_space=pltpu.HBM)
        rows, points = charges.shape
        dma = pltpu.SemaphoreType.DMA
        return pl.pallas_call(
            functools.partial(kernel, dims),
            out_shape=jax.ShapeDtypeStruct(charges.shape, bf),
            in_specs=[hbm] * 9,
            out_specs=vmem,
            scratch_shapes=[
                pltpu.SMEM(wanted.shape[2:], jnp.int32),
                pltpu.SMEM(far_source.shape, jnp.int32),
                pltpu.VMEM(charges.shape, bf),
                pltpu.VMEM(positions.shape, bf),
                pltpu.VMEM(bases.shape, bf),
                pltpu.VMEM(transfers.shape, bf),
                pltpu.VMEM(couplings.shape[:0:-1], bf),
                pltpu.VMEM(near_target.shape[1:], jnp.int32),
                pltpu.VMEM(near_slot.shape[1:], jnp.int32),
                dma((9,)),
            ]
            + [pltpu.VMEM((LEAVES, rows, BS), bf)] * 8
            + [pltpu.VMEM((3 * LEAVES, BS), bf)] * 8
            + [
                pltpu.VMEM((3 * LEAVES, BS), f32),
                pltpu.VMEM((FEATS, points), bf),
                pltpu.VMEM((LEAVES, FEATS, BS), f32),
                pltpu.VMEM((FEATS, CAP * BS), f32),
                pltpu.VMEM((CAP * BS, FEATS), bf),
                pltpu.VMEM((rows, CAP * BS), bf),
                pltpu.VMEM((GRP, CAP, points), f32),
                pltpu.VMEM((rows, points), f32),
                pltpu.VMEM((GRP, 32, 128), bf),
                pltpu.VMEM((GRP, 32, 128), bf),
                pltpu.VMEM((X * Z * C, 32, 128), bf),
                dma((2, 7)),
                dma((2, 7)),
                dma((2, 4)),
                dma((2, 4)),
                dma((GRP,)),
                dma((GRP,)),
                dma((GRP,)),
                dma((GRP,)),
                dma((2, Z)),
                dma((2, Z)),
                dma((X,)),
                dma((X,)),
                dma,
                dma,
                pltpu.SemaphoreType.REGULAR,
            ],
            compiler_params=pltpu.CompilerParams(
                collective_id=0, has_side_effects=True, vmem_limit_bytes=56 << 20
            ),
        )(
            wanted[0, 0],
            far_source,
            charges,
            positions,
            bases,
            transfers,
            jnp.swapaxes(couplings[0], 0, 1),
            near_target[0],
            near_slot[0],
        )

    in_specs = (
        P(None, ("leaf", "grp")),
        P(None, ("leaf", "grp")),
        P(None, ("leaf", "grp")),
        P(("leaf", "grp"), None, None),
        P("leaf", "grp", None),
        P("leaf", None),
        P("leaf", "grp", None, None),
        P("leaf", "grp", None),
        P("leaf", "grp", None),
    )
    out_specs = P(None, ("leaf", "grp"))
    return jax.shard_map(shards, mesh=mesh, in_specs=in_specs, out_specs=out_specs, check_vma=False)
```

```python
import functools

import jax
import jax.numpy as jnp
from jax import lax
from jax.experimental import pallas as pl
from jax.experimental.pallas import tpu as pltpu
from jax.sharding import PartitionSpec as P

MESH = pl.DeviceIdType.MESH
bf = jnp.bfloat16
f32 = jnp.float32
GRP = 8
LEAVES = 16
BS = 128
CAP = 8
HALF = LEAVES // 2
FEATS = 16
QUARTERS = 4
ROWS = 16
SOFTEN2 = 0.05 * 0.05
SCALE = float(BS * BS)
NT = (((1,), (1,)), ((), ()))


def dot_nt(a, b):
    return lax.dot_general(a, b, NT, preferred_element_type=f32)


def dot(a, b):
    return jnp.dot(a, b, preferred_element_type=f32)


def pack(x):
    return jnp.concatenate([x[:32, :], x[32:, :]], axis=1)


def unpack(x):
    return jnp.concatenate([x[:, :64], x[:, 64:]], axis=0)


def pieces(n):
    high = n.astype(bf).astype(f32)
    rest = n - high
    middle = rest.astype(bf).astype(f32)
    return high, middle, rest - middle


def kernel(
    dims,
    wanted_in,
    far_source_in,
    charges_in,
    positions_in,
    bases_in,
    transfers_in,
    couplings_in,
    near_target_in,
    near_slot_in,
    out,
    wanted,
    far_source,
    charges,
    positions,
    bases,
    transfers,
    near_target,
    near_slot,
    in_sem,
    ch0,
    ch1,
    ch2,
    ch3,
    ch4,
    ch5,
    ch6,
    ch7,
    ps0,
    ps1,
    ps2,
    ps3,
    ps4,
    ps5,
    ps6,
    ps7,
    pos_rows,
    target_feat,
    source_feat,
    feat_sel,
    feat_sel_t,
    charge_sel,
    weight,
    acc,
    up_out,
    part_up,
    sibling,
    part_down,
    coeffs,
    panels,
    ring_send,
    ring_recv,
    pos_send,
    pos_recv,
    up_send,
    up_recv,
    down_send,
    down_recv,
    z_send,
    z_recv,
    x_send,
    x_recv,
    core_send,
    core_recv,
    panel_send,
    panel_recv,
    ready,
):
    X, Z, C = dims
    leaf = lax.axis_index("leaf")
    y = lax.axis_index("grp")
    x = leaf // (Z * C)
    z = (leaf // C) % Z
    core = leaf % C
    quarter = y % QUARTERS
    first_y = y - quarter
    chunk = [ch0, ch1, ch2, ch3, ch4, ch5, ch6, ch7]
    place = [ps0, ps1, ps2, ps3, ps4, ps5, ps6, ps7]

    def y_peer(k):
        return (leaf, (y + k) % GRP)

    def z_peer(k):
        return ((x * Z + (z + k) % Z) * C + core, y)

    def x_peer(k):
        return ((((x + k) % X) * Z + z) * C + core, y)

    core_peer = ((x * Z + z) * C + (1 - core), y)

    ins = [
        (charges_in, charges),
        (positions_in, positions),
        (bases_in, bases),
        (transfers_in, transfers),
        (near_target_in, near_target),
        (near_slot_in, near_slot),
        (wanted_in, wanted),
        (far_source_in, far_source),
        (couplings_in.at[pl.ds(pl.multiple_of(quarter * ROWS, ROWS), ROWS)], panels.at[0]),
    ]

    def fetch(i):
        return pltpu.make_async_copy(ins[i][0], ins[i][1], in_sem.at[i])

    for i in range(len(ins)):
        fetch(i).start()

    barrier = pltpu.get_barrier_semaphore()

    def greet(peer):
        pl.semaphore_signal(barrier, inc=1, device_id=peer, device_id_type=MESH)

    for k in range(1, GRP):
        greet(y_peer(k))
    for k in range(1, X):
        greet(x_peer(k))
    if C > 1:
        greet(core_peer)
    for k in range(1, Z):

        @pl.when(z + k < Z)
        def _():
            greet(z_peer(k))

    for i in range(4):
        fetch(i).wait()

    pos = positions[...].astype(f32)
    for d in range(3):
        for t in range(LEAVES):
            row = d * LEAVES + t
            pos_rows[row : row + 1, :] = pos[d : d + 1, t * BS : (t + 1) * BS]
    ps0[...] = pos_rows[...].astype(bf)
    for t in range(LEAVES):
        ch0[t] = charges[:, t * BS : (t + 1) * BS]

    partial = None
    for t in range(LEAVES):
        cols = slice(t * BS, (t + 1) * BS)
        leaf_coeff = dot_nt(bases[:, cols], charges[:, cols]).astype(bf)
        term = dot(transfers[t], leaf_coeff)
        partial = term if partial is None else partial + term
    partial = jnp.concatenate([partial, partial], axis=1).astype(bf)
    for q in range(QUARTERS):
        up_out[q] = partial[q * ROWS : (q + 1) * ROWS, :]

    pl.semaphore_wait(barrier, (GRP - 1) + (X - 1) + (C - 1) + z)
    for k in range(1, Z):

        @pl.when(k <= z)
        def _():
            pl.semaphore_signal(ready, inc=1, device_id=z_peer(Z - k), device_id_type=MESH)


    def up_copy(k):
        return pltpu.make_async_remote_copy(
            src_ref=up_out.at[(y + k) % QUARTERS],
            dst_ref=part_up.at[k],
            send_sem=up_send.at[k],
            recv_sem=up_recv.at[k],
            device_id=y_peer(k),
            device_id_type=MESH,
        )

    def down_copy(k):
        return pltpu.make_async_remote_copy(
            src_ref=part_down.at[0],
            dst_ref=part_down.at[k],
            send_sem=down_send.at[k],
            recv_sem=down_recv.at[k],
            device_id=y_peer(k),
            device_id_type=MESH,
        )

    def panel_copy(k):
        to = (quarter + k) % QUARTERS
        return pltpu.make_async_remote_copy(
            src_ref=couplings_in.at[pl.ds(pl.multiple_of(to * ROWS, ROWS), ROWS)],
            dst_ref=panels.at[k],
            send_sem=panel_send.at[k],
            recv_sem=panel_recv.at[k],
            device_id=(leaf, first_y + to),
            device_id_type=MESH,
        )

    def ring(right, step, half):
        src = step if right else (GRP - step) % GRP
        dst = step + 1 if right else GRP - step - 1
        part = pl.ds(half * HALF, HALF)
        way = 0 if right else 1
        slot = 2 * step + (half if step < 3 else 0)
        return pltpu.make_async_remote_copy(
            src_ref=chunk[src].at[part],
            dst_ref=chunk[dst].at[part],
            send_sem=ring_send.at[way, slot],
            recv_sem=ring_recv.at[way, slot],
            device_id=y_peer(1 if right else GRP - 1),
            device_id_type=MESH,
        )

    def ring_pos(right, step):
        src = step if right else (GRP - step) % GRP
        dst = step + 1 if right else GRP - step - 1
        way = 0 if right else 1
        return pltpu.make_async_remote_copy(
            src_ref=place[src],
            dst_ref=place[dst],
            send_sem=pos_send.at[way, step],
            recv_sem=pos_recv.at[way, step],
            device_id=y_peer(1 if right else GRP - 1),
            device_id_type=MESH,
        )

    def slot_of(x_at, z_at):
        return x_at * Z + z_at

    def z_copy(up, k, z_at):
        here = coeffs.at[slot_of(x, z_at)]
        return pltpu.make_async_remote_copy(
            src_ref=here,
            dst_ref=here,
            send_sem=z_send.at[up, k],
            recv_sem=z_recv.at[up, k],
            device_id=z_peer(k if up else Z - k),
            device_id_type=MESH,
        )

    def each_z(up, do):
        for k in range(1, Z):

            @pl.when(z + k < Z if up else k <= z)
            def _():
                do(k)

    def x_copy(k, x_at):
        here = coeffs.at[pl.ds(slot_of(x_at, 0), Z)]
        return pltpu.make_async_remote_copy(
            src_ref=here,
            dst_ref=here,
            send_sem=x_send.at[k],
            recv_sem=x_recv.at[k],
            device_id=x_peer(k),
            device_id_type=MESH,
        )

    def core_copy():
        return pltpu.make_async_remote_copy(
            src_ref=sibling.at[0],
            dst_ref=sibling.at[1],
            send_sem=core_send,
            recv_sem=core_recv,
            device_id=core_peer,
            device_id_type=MESH,
        )

    for k in range(1, GRP):
        up_copy(k).start()
    for right in (True, False):
        ring_pos(right, 0).start()
    for half in (0, 1):
        for right in (True, False):
            ring(right, 0, half).start()

    norm = jnp.sum(pos * pos, axis=0, keepdims=True) + SOFTEN2
    high, middle, low = pieces(norm)
    one = jnp.ones_like(norm)
    target_feat[...] = (
        jnp.concatenate(
            [-2.0 * pos, high, middle, low, one, one, one, jnp.zeros((FEATS - 9, norm.shape[1]), f32)],
            axis=0,
        )
        * SCALE
    ).astype(bf)
    source_feat[...] = jnp.zeros_like(source_feat)
    for f in (3, 4, 5):
        source_feat[:, f, :] = jnp.ones((LEAVES, BS), f32)

    for i in range(4, 8):
        fetch(i).wait()

    blocks = near_slot.shape[1]
    slot_hot = (
        lax.broadcasted_iota(jnp.int32, (GRP * CAP, blocks), 0) == near_slot[...]
    ).astype(f32)
    leaf_hot = (
        lax.broadcasted_iota(jnp.int32, (LEAVES, blocks), 0) == near_target[...]
    ).astype(f32)
    counts = dot_nt(slot_hot.astype(bf), leaf_hot.astype(bf))
    spread = (
        lax.broadcasted_iota(jnp.int32, (LEAVES, LEAVES * BS), 1) // BS
        == lax.broadcasted_iota(jnp.int32, (LEAVES, LEAVES * BS), 0)
    ).astype(f32)
    spread_counts = dot(counts.astype(bf), spread.astype(bf))
    for h in range(GRP):
        weight[h] = spread_counts[h * CAP : (h + 1) * CAP, :]

    def near(rel, first=False):
        h = (y + (GRP - rel)) % GRP
        rows = place[rel][...].astype(f32)
        px, py, pz = rows[0:16], rows[16:32], rows[32:48]
        parts = pieces(px * px + py * py + pz * pz)
        for f, v in zip((0, 1, 2, 6, 7, 8), (px, py, pz) + parts):
            source_feat[:, f, :] = v
        for c in range(CAP):
            at = wanted[h, c]
            cols = slice(c * BS, (c + 1) * BS)
            charge_sel[:, cols] = chunk[rel][at]
            feat_sel[:, cols] = source_feat[at]
        feat_sel_t[...] = feat_sel[...].T.astype(bf)
        width, depth = 1024, 512

        def block(i, carry):
            cols = pl.ds(pl.multiple_of(i * width, width), width)
            targets = target_feat[:, cols]
            w = weight[h, :, cols].astype(bf)
            total = None
            for k in range(0, CAP * BS, depth):
                dist = dot(feat_sel_t[k : k + depth, :], targets)
                g = lax.rsqrt(dist.astype(bf))
                g = jnp.concatenate(
                    [
                        g[j * BS : (j + 1) * BS, :] * w[k // BS + j : k // BS + j + 1, :]
                        for j in range(depth // BS)
                    ],
                    axis=0,
                )
                term = dot(charge_sel[:, k : k + depth], g)
                total = term if total is None else total + term
            if not first:
                total = total + acc[:, cols]
            acc[:, cols] = total
            return carry

        lax.fori_loop(0, LEAVES * BS // width, block, 0)

    def arrived(step, half, right=True, left=True):
        for way in (True, False):
            if (right if way else left):
                if half == 0 or step == 3:
                    if not (step == 3 and not way):
                        ring_pos(way, step).wait_recv()
                        if step < 2 or (step == 2 and way):
                            ring_pos(way, step + 1).start()
                ring(way, step, half).wait_recv()
                if step < 2:
                    ring(way, step + 1, half).start()
                elif step == 2 and (half == 0) == way:
                    ring(way, 3, half).start()

    near(0, first=True)

    for k in range(1, GRP):
        up_copy(k).wait_recv()
    total = up_out[quarter].astype(f32)
    for k in range(1, GRP):
        total = total + part_up[k].astype(f32)
    if C > 1:
        sibling[0] = total.astype(bf)
        core_copy().start()
    arrived(0, 0)
    if C > 1:
        core_copy().wait_recv()
        side = lax.broadcasted_iota(jnp.int32, total.shape, 1) // (total.shape[1] // 2)
        total = jnp.where(side == core, total.astype(bf).astype(f32), sibling[1].astype(f32))
    coeffs[slot_of(x, z)] = total.astype(bf)
    each_z(0, lambda k: z_copy(0, k, z).start())

    arrived(0, 1)
    for k in range(1, QUARTERS):
        panel_copy(k).start()
    near(1)
    arrived(1, 0)
    near(7)
    arrived(1, 1)
    near(2)
    arrived(2, 0)

    @pl.when(z < Z - 1)
    def _():
        pl.semaphore_wait(ready, Z - 1 - z)

    each_z(1, lambda k: z_copy(1, k, z).start())
    near(6)
    arrived(2, 1)
    each_z(1, lambda k: z_copy(0, k, z + k).wait_recv())
    each_z(0, lambda k: z_copy(1, k, z - k).wait_recv())
    for k in range(1, X):
        x_copy(k, x).start()
    near(3)
    near(5)

    for k in range(1, X):
        x_copy(k, (x + (X - k)) % X).wait_recv()
    fetch(8).wait()
    for k in range(1, QUARTERS):
        panel_copy(k).wait_recv()
    rank = couplings_in.shape[0]
    count = couplings_in.shape[1] // rank
    terms = []
    for odd in (0, 1):
        coeff_rows, panel_rows = [], []
        for k in range(QUARTERS):
            owner = first_y + (quarter + (QUARTERS - k)) % QUARTERS
            for j in range(odd, count, 2):
                source = far_source[0, owner * count + j]
                if C == 1:
                    rows = coeffs[source].astype(f32)[:, :rank]
                else:
                    both = coeffs[source >> 1].astype(f32)
                    rows = jnp.where((source & 1) == 0, both[:, :rank], both[:, rank:])
                coeff_rows.append(rows)
                panel_rows.append(panels[k, :, (j - odd) * rank : (j - odd + 2) * rank])
        left = jnp.concatenate(coeff_rows, axis=0).T.astype(bf)
        terms.append(dot(left, jnp.concatenate(panel_rows, axis=0)))
    part_down[0] = pack(terms[0][:, :rank] + terms[1][:, rank:]).astype(bf)
    for k in range(1, GRP):
        down_copy(k).start()

    arrived(3, 0, left=False)
    arrived(3, 1, right=False)
    near(4)

    for k in range(1, GRP):
        down_copy(k).wait_recv()
    total = part_down[0].astype(f32)
    for k in range(1, GRP):
        total = total + part_down[k].astype(f32)
    target_coeff = unpack(total.astype(bf))
    for t in range(LEAVES):
        cols = slice(t * BS, (t + 1) * BS)
        leaf_target = dot(target_coeff, transfers[t]).astype(bf)
        out[:, cols] = (acc[:, cols] + dot(leaf_target, bases[:, cols])).astype(bf)

    for k in range(1, GRP):
        up_copy(k).wait_send()
        down_copy(k).wait_send()
    for right in (True, False):
        for step in range(3):
            ring_pos(right, step).wait_send()
            for half in (0, 1):
                ring(right, step, half).wait_send()
    ring_pos(True, 3).wait_send()
    ring(True, 3, 0).wait_send()
    ring(False, 3, 1).wait_send()
    for up in (0, 1):
        each_z(up, lambda k: z_copy(up, k, z).wait_send())
    for k in range(1, X):
        x_copy(k, x).wait_send()
    for k in range(1, QUARTERS):
        panel_copy(k).wait_send()
    if C > 1:
        core_copy().wait_send()


def solution(mesh):
    n_leaf = mesh.shape["leaf"]
    dims = {128: (4, 16, 2), 1: (1, 1, 1), 2: (1, 1, 2), 8: (2, 2, 2), 16: (2, 4, 2)}[n_leaf]
    X, Z, C = dims

    def shards(charges, positions, bases, transfers, couplings, far_source, wanted, near_target, near_slot):
        vmem = pl.BlockSpec(memory_space=pltpu.VMEM)
        hbm = pl.BlockSpec(memory_space=pltpu.HBM)
        rows, points = charges.shape
        dma = pltpu.SemaphoreType.DMA
        return pl.pallas_call(
            functools.partial(kernel, dims),
            out_shape=jax.ShapeDtypeStruct(charges.shape, bf),
            in_specs=[hbm] * 9,
            out_specs=vmem,
            scratch_shapes=[
                pltpu.SMEM(wanted.shape[2:], jnp.int32),
                pltpu.SMEM(far_source.shape, jnp.int32),
                pltpu.VMEM(charges.shape, bf),
                pltpu.VMEM(positions.shape, bf),
                pltpu.VMEM(bases.shape, bf),
                pltpu.VMEM(transfers.shape, bf),
                pltpu.VMEM(near_target.shape[1:], jnp.int32),
                pltpu.VMEM(near_slot.shape[1:], jnp.int32),
                dma((9,)),
            ]
            + [pltpu.VMEM((LEAVES, rows, BS), bf)] * 8
            + [pltpu.VMEM((3 * LEAVES, BS), bf)] * 8
            + [
                pltpu.VMEM((3 * LEAVES, BS), f32),
                pltpu.VMEM((FEATS, points), bf),
                pltpu.VMEM((LEAVES, FEATS, BS), f32),
                pltpu.VMEM((FEATS, CAP * BS), f32),
                pltpu.VMEM((CAP * BS, FEATS), bf),
                pltpu.VMEM((rows, CAP * BS), bf),
                pltpu.VMEM((GRP, CAP, points), f32),
                pltpu.VMEM((rows, points), f32),
                pltpu.VMEM((QUARTERS, ROWS, 128), bf),
                pltpu.VMEM((GRP, ROWS, 128), bf),
                pltpu.VMEM((2, ROWS, 128), bf),
                pltpu.VMEM((GRP, 32, 128), bf),
                pltpu.VMEM((X * Z, ROWS, 128), bf),
                pltpu.VMEM((QUARTERS, ROWS, couplings.shape[1]), bf),
                dma((2, 7)),
                dma((2, 7)),
                dma((2, 4)),
                dma((2, 4)),
                dma((GRP,)),
                dma((GRP,)),
                dma((GRP,)),
                dma((GRP,)),
                dma((2, Z)),
                dma((2, Z)),
                dma((X,)),
                dma((X,)),
                dma,
                dma,
                dma((QUARTERS,)),
                dma((QUARTERS,)),
                pltpu.SemaphoreType.REGULAR,
            ],
            compiler_params=pltpu.CompilerParams(
                collective_id=0, has_side_effects=True, vmem_limit_bytes=56 << 20
            ),
        )(
            wanted[0, 0],
            far_source,
            charges,
            positions,
            bases,
            transfers,
            jnp.swapaxes(couplings[0], 0, 1),
            near_target[0],
            near_slot[0],
        )

    in_specs = (
        P(None, ("leaf", "grp")),
        P(None, ("leaf", "grp")),
        P(None, ("leaf", "grp")),
        P(("leaf", "grp"), None, None),
        P("leaf", "grp", None),
        P("leaf", None),
        P("leaf", "grp", None, None),
        P("leaf", "grp", None),
        P("leaf", "grp", None),
    )
    out_specs = P(None, ("leaf", "grp"))
    return jax.shard_map(shards, mesh=mesh, in_specs=in_specs, out_specs=out_specs, check_vma=False)
```

```python
import functools

import jax
import jax.numpy as jnp
from jax import lax
from jax.experimental import pallas as pl
from jax.experimental.pallas import tpu as pltpu
from jax.sharding import PartitionSpec as P

MESH = pl.DeviceIdType.MESH
bf = jnp.bfloat16
f32 = jnp.float32
GRP = 8
LEAVES = 16
BS = 128
CAP = 8
HALF = LEAVES // 2
FEATS = 9
LANES = 256
QUARTERS = 4
ROWS = 16
SOFTEN2 = 0.05 * 0.05
SCALE = float(BS * BS)
NT = (((1,), (1,)), ((), ()))


def dot_nt(a, b):
    return lax.dot_general(a, b, NT, preferred_element_type=f32)


def dot(a, b):
    return jnp.dot(a, b, preferred_element_type=f32)


def pack(x):
    return jnp.concatenate([x[:32, :], x[32:, :]], axis=1)


def unpack(x):
    return jnp.concatenate([x[:, :64], x[:, 64:]], axis=0)


def pieces(n):
    high = n.astype(bf).astype(f32)
    rest = n - high
    middle = rest.astype(bf).astype(f32)
    return high, middle, rest - middle


def kernel(
    dims,
    wanted_in,
    far_source_in,
    charges_in,
    positions_in,
    bases_in,
    transfers_in,
    couplings_in,
    near_target_in,
    near_slot_in,
    out,
    wanted,
    far_source,
    charges,
    positions,
    bases,
    transfers,
    near_target,
    near_slot,
    in_sem,
    ch0,
    ch1,
    ch2,
    ch3,
    ch4,
    ch5,
    ch6,
    ch7,
    ps0,
    ps1,
    ps2,
    ps3,
    ps4,
    ps5,
    ps6,
    ps7,
    pos_rows,
    target_feat,
    feat_sel,
    charge_sel,
    weight,
    acc,
    up_out,
    part_up,
    sibling,
    part_down,
    coeffs,
    panels,
    ring_send,
    ring_recv,
    pos_send,
    pos_recv,
    up_send,
    up_recv,
    down_send,
    down_recv,
    z_send,
    z_recv,
    x_send,
    x_recv,
    core_send,
    core_recv,
    panel_send,
    panel_recv,
    ready_z,
    ready_x,
    ready_core,
):
    X, Z, C = dims
    leaf = lax.axis_index("leaf")
    y = lax.axis_index("grp")
    x = leaf // (Z * C)
    z = (leaf // C) % Z
    core = leaf % C
    quarter = y % QUARTERS
    first_y = y - quarter
    chunk = [ch0, ch1, ch2, ch3, ch4, ch5, ch6, ch7]
    place = [ps0, ps1, ps2, ps3, ps4, ps5, ps6, ps7]

    def y_peer(k):
        return (leaf, (y + k) % GRP)

    def z_peer(k):
        return ((x * Z + (z + k) % Z) * C + core, y)

    def x_peer(k):
        return ((((x + k) % X) * Z + z) * C + core, y)

    core_peer = ((x * Z + z) * C + (1 - core), y)

    ins = [
        (charges_in, charges),
        (positions_in, positions),
        (bases_in, bases),
        (transfers_in, transfers),
        (near_target_in, near_target),
        (near_slot_in, near_slot),
        (wanted_in, wanted),
        (far_source_in, far_source),
        (couplings_in.at[pl.ds(pl.multiple_of(quarter * ROWS, ROWS), ROWS)], panels.at[0]),
    ]

    def fetch(i):
        return pltpu.make_async_copy(ins[i][0], ins[i][1], in_sem.at[i])

    for i in range(len(ins)):
        fetch(i).start()

    barrier = pltpu.get_barrier_semaphore()

    def greet(peer):
        pl.semaphore_signal(barrier, inc=1, device_id=peer, device_id_type=MESH)

    first_column = (x + y + core) == 0

    def order(z_at):
        return jnp.where(first_column & (z_at == 0), Z - 1, 2 * z_at)

    def z_speaks(k):
        return order(z) < order((z + k) % Z)

    def answer(semaphore, peer):
        pl.semaphore_signal(semaphore, inc=1, device_id=peer, device_id_type=MESH)

    for k in range(1, GRP):
        greet(y_peer(k))
    if C > 1:

        @pl.when(core == 1)
        def _():
            greet(core_peer)

    for k in range(1, X):

        @pl.when(x >= k)
        def _():
            greet(x_peer(X - k))

    for k in range(1, Z):

        @pl.when(z_speaks(k))
        def _():
            greet(z_peer(k))

    heard_z = sum([jnp.where(z_speaks(k), 0, 1) for k in range(1, Z)], 0)

    fetch(0).wait()
    fetch(1).wait()

    pos = positions[...].astype(f32)
    for d in range(3):
        for t in range(LEAVES):
            row = d * LEAVES + t
            pos_rows[row : row + 1, :] = pos[d : d + 1, t * BS : (t + 1) * BS]
    ps0[...] = pos_rows[...].astype(bf)
    for t in range(LEAVES):
        ch0[t] = charges[:, t * BS : (t + 1) * BS]

    pl.semaphore_wait(barrier, (GRP - 1) + (X - 1 - x) + (C - 1) * (1 - core) + heard_z)

    def up_copy(k):
        return pltpu.make_async_remote_copy(
            src_ref=up_out.at[(y + k) % QUARTERS],
            dst_ref=part_up.at[k],
            send_sem=up_send.at[k],
            recv_sem=up_recv.at[k],
            device_id=y_peer(k),
            device_id_type=MESH,
        )

    def down_copy(k):
        return pltpu.make_async_remote_copy(
            src_ref=part_down.at[0],
            dst_ref=part_down.at[k],
            send_sem=down_send.at[k],
            recv_sem=down_recv.at[k],
            device_id=y_peer(k),
            device_id_type=MESH,
        )

    def panel_copy(k):
        to = (quarter + k) % QUARTERS
        return pltpu.make_async_remote_copy(
            src_ref=couplings_in.at[pl.ds(pl.multiple_of(to * ROWS, ROWS), ROWS)],
            dst_ref=panels.at[k],
            send_sem=panel_send.at[k],
            recv_sem=panel_recv.at[k],
            device_id=(leaf, first_y + to),
            device_id_type=MESH,
        )

    def ring(right, step, half):
        src = step if right else (GRP - step) % GRP
        dst = step + 1 if right else GRP - step - 1
        part = pl.ds(half * HALF, HALF)
        way = 0 if right else 1
        slot = 2 * step + (half if step < 3 else 0)
        return pltpu.make_async_remote_copy(
            src_ref=chunk[src].at[part],
            dst_ref=chunk[dst].at[part],
            send_sem=ring_send.at[way, slot],
            recv_sem=ring_recv.at[way, slot],
            device_id=y_peer(1 if right else GRP - 1),
            device_id_type=MESH,
        )

    def ring_pos(right, step):
        src = step if right else (GRP - step) % GRP
        dst = step + 1 if right else GRP - step - 1
        way = 0 if right else 1
        return pltpu.make_async_remote_copy(
            src_ref=place[src],
            dst_ref=place[dst],
            send_sem=pos_send.at[way, step],
            recv_sem=pos_recv.at[way, step],
            device_id=y_peer(1 if right else GRP - 1),
            device_id_type=MESH,
        )

    def slot_of(x_at, z_at):
        return x_at * Z + z_at

    def z_copy(k, z_at):
        here = coeffs.at[slot_of(x, z_at)]
        return pltpu.make_async_remote_copy(
            src_ref=here,
            dst_ref=here,
            send_sem=z_send.at[k],
            recv_sem=z_recv.at[k],
            device_id=z_peer(k),
            device_id_type=MESH,
        )

    def each_z(speaks, do):
        for k in range(1, Z):

            @pl.when(z_speaks(k) if speaks else jnp.logical_not(z_speaks(k)))
            def _():
                do(k)

    def x_copy(k, x_at):
        here = coeffs.at[pl.ds(slot_of(x_at, 0), Z)]
        return pltpu.make_async_remote_copy(
            src_ref=here,
            dst_ref=here,
            send_sem=x_send.at[k],
            recv_sem=x_recv.at[k],
            device_id=x_peer(k),
            device_id_type=MESH,
        )

    def core_copy():
        return pltpu.make_async_remote_copy(
            src_ref=sibling.at[0],
            dst_ref=sibling.at[1],
            send_sem=core_send,
            recv_sem=core_recv,
            device_id=core_peer,
            device_id_type=MESH,
        )

    for right in (True, False):
        ring_pos(right, 0).start()
        ring(right, 0, 0).start()

    if C > 1:

        @pl.when(core == 0)
        def _():
            answer(ready_core, core_peer)

    for k in range(1, X):

        @pl.when(x + k < X)
        def _():
            answer(ready_x, x_peer(k))

    each_z(False, lambda k: answer(ready_z, z_peer(k)))

    fetch(2).wait()
    fetch(3).wait()
    partial = None
    for t in range(LEAVES):
        cols = slice(t * BS, (t + 1) * BS)
        leaf_coeff = dot_nt(bases[:, cols], charges[:, cols]).astype(bf)
        term = dot(transfers[t], leaf_coeff)
        partial = term if partial is None else partial + term
    partial = jnp.concatenate([partial, partial], axis=1).astype(bf)
    for q in range(QUARTERS):
        up_out[q] = partial[q * ROWS : (q + 1) * ROWS, :]
    for k in range(1, GRP):
        up_copy(k).start()
    for right in (True, False):
        ring(right, 0, 1).start()

    norm = jnp.sum(pos * pos, axis=0, keepdims=True) + SOFTEN2
    high, middle, low = pieces(norm)
    one = jnp.ones_like(norm)
    target_feat[...] = jnp.zeros_like(target_feat)
    for f, v in enumerate((-2.0 * pos[0:1], -2.0 * pos[1:2], -2.0 * pos[2:3], high, middle, low, one, one, one)):
        rows = jnp.broadcast_to(v * SCALE, (LEAVES, v.shape[1]))
        target_feat[f * LEAVES : (f + 1) * LEAVES, :] = rows.astype(bf)

    for i in range(4, 8):
        fetch(i).wait()

    blocks = near_slot.shape[1]
    slot_hot = (
        lax.broadcasted_iota(jnp.int32, (GRP * CAP, blocks), 0) == near_slot[...]
    ).astype(f32)
    leaf_hot = (
        lax.broadcasted_iota(jnp.int32, (LEAVES, blocks), 0) == near_target[...]
    ).astype(f32)
    counts = dot_nt(slot_hot.astype(bf), leaf_hot.astype(bf))
    spread = (
        lax.broadcasted_iota(jnp.int32, (LEAVES, LEAVES * BS), 1) // BS
        == lax.broadcasted_iota(jnp.int32, (LEAVES, LEAVES * BS), 0)
    ).astype(f32)
    spread_counts = dot(counts.astype(bf), spread.astype(bf))
    for h in range(GRP):
        weight[h] = spread_counts[h * CAP : (h + 1) * CAP, :]

    def near(rel, first=False, last=False):
        h = (y + (GRP - rel)) % GRP
        rows = place[rel][...].astype(f32)
        px, py, pz = rows[0:16], rows[16:32], rows[32:48]
        ones = jnp.ones_like(px)
        parts = pieces(px * px + py * py + pz * pz)
        pad = jnp.zeros((LANES - FEATS * LEAVES, BS), f32)
        feats = jnp.concatenate((px, py, pz, ones, ones, ones) + parts + (pad,), axis=0)
        feats = feats.T
        lane_leaf = lax.broadcasted_iota(jnp.int32, feats.shape, 1) % LEAVES
        for c in range(CAP):
            at = wanted[h, c]
            charge_sel[:, c * BS : (c + 1) * BS] = chunk[rel][at]
            feat_sel[c * BS : (c + 1) * BS, :] = jnp.where(lane_leaf == at, feats, 0.0).astype(bf)
        depth = 256
        total = None if first else acc[...]
        w = weight[h].astype(bf)
        for k in range(0, CAP * BS, depth):
            dist = dot(feat_sel[k : k + depth, :], target_feat[...])
            g = lax.rsqrt(dist.astype(bf))
            g = jnp.concatenate(
                [
                    g[j * BS : (j + 1) * BS, :] * w[k // BS + j : k // BS + j + 1, :]
                    for j in range(depth // BS)
                ],
                axis=0,
            )
            term = dot(charge_sel[:, k : k + depth], g)
            total = term if total is None else total + term
        if last:
            out[...] = total.astype(bf)
        else:
            acc[...] = total

    def arrived(step, half, right=True, left=True):
        for way in (True, False):
            if (right if way else left):
                if half == 0 or step == 3:
                    if not (step == 3 and not way):
                        ring_pos(way, step).wait_recv()
                        if step < 2 or (step == 2 and way):
                            ring_pos(way, step + 1).start()
                ring(way, step, half).wait_recv()
                if step < 2:
                    ring(way, step + 1, half).start()
                elif step == 2 and (half == 0) == way:
                    ring(way, 3, half).start()

    for k in range(1, GRP):
        up_copy(k).wait_recv()
    total = up_out[quarter].astype(f32)
    for k in range(1, GRP):
        total = total + part_up[k].astype(f32)
    if C > 1:
        sibling[0] = total.astype(bf)

        @pl.when(core == 1)
        def _():
            pl.semaphore_wait(ready_core, 1)

        core_copy().start()
    arrived(0, 0)
    if C > 1:
        core_copy().wait_recv()
        side = lax.broadcasted_iota(jnp.int32, total.shape, 1) // (total.shape[1] // 2)
        total = jnp.where(side == core, total.astype(bf).astype(f32), sibling[1].astype(f32))
    coeffs[slot_of(x, z)] = total.astype(bf)
    each_z(False, lambda k: z_copy(k, z).start())

    near(0, first=True)
    arrived(0, 1)
    for k in range(1, QUARTERS):
        panel_copy(k).start()
    near(1)
    arrived(1, 0)
    near(7)
    arrived(1, 1)

    @pl.when(heard_z < Z - 1)
    def _():
        pl.semaphore_wait(ready_z, Z - 1 - heard_z)

    each_z(True, lambda k: z_copy(k, z).start())
    near(2)
    for k in range(1, Z):
        z_copy(k, (z + (Z - k)) % Z).wait_recv()

    @pl.when(x > 0)
    def _():
        pl.semaphore_wait(ready_x, x)

    for k in range(1, X):
        x_copy(k, x).start()
    arrived(2, 0)
    near(6)

    for k in range(1, X):
        x_copy(k, (x + (X - k)) % X).wait_recv()
    fetch(8).wait()
    for k in range(1, QUARTERS):
        panel_copy(k).wait_recv()
    rank = couplings_in.shape[0]
    count = couplings_in.shape[1] // rank
    terms = []
    for odd in (0, 1):
        coeff_rows, panel_rows = [], []
        for k in range(QUARTERS):
            owner = first_y + (quarter + (QUARTERS - k)) % QUARTERS
            for j in range(odd, count, 2):
                source = far_source[0, owner * count + j]
                if C == 1:
                    rows = coeffs[source].astype(f32)[:, :rank]
                else:
                    both = coeffs[source >> 1].astype(f32)
                    rows = jnp.where((source & 1) == 0, both[:, :rank], both[:, rank:])
                coeff_rows.append(rows)
                panel_rows.append(panels[k, :, (j - odd) * rank : (j - odd + 2) * rank])
        left = jnp.concatenate(coeff_rows, axis=0).T.astype(bf)
        terms.append(dot(left, jnp.concatenate(panel_rows, axis=0)))
    part_down[0] = pack(terms[0][:, :rank] + terms[1][:, rank:]).astype(bf)
    for k in range(1, GRP):
        down_copy(k).start()

    arrived(2, 1)
    near(3)
    near(5)

    for k in range(1, GRP):
        down_copy(k).wait_recv()
    total = part_down[0].astype(f32)
    for k in range(1, GRP):
        total = total + part_down[k].astype(f32)
    target_coeff = unpack(total.astype(bf))
    for t in range(LEAVES):
        cols = slice(t * BS, (t + 1) * BS)
        leaf_target = dot(target_coeff, transfers[t]).astype(bf)
        acc[:, cols] += dot(leaf_target, bases[:, cols])

    arrived(3, 0, left=False)
    arrived(3, 1, right=False)
    near(4, last=True)

    for k in range(1, GRP):
        up_copy(k).wait_send()
        down_copy(k).wait_send()
    for right in (True, False):
        for step in range(3):
            ring_pos(right, step).wait_send()
            for half in (0, 1):
                ring(right, step, half).wait_send()
    ring_pos(True, 3).wait_send()
    ring(True, 3, 0).wait_send()
    ring(False, 3, 1).wait_send()
    for k in range(1, Z):
        z_copy(k, z).wait_send()
    for k in range(1, X):
        x_copy(k, x).wait_send()
    for k in range(1, QUARTERS):
        panel_copy(k).wait_send()
    if C > 1:
        core_copy().wait_send()


def solution(mesh):
    n_leaf = mesh.shape["leaf"]
    dims = {128: (4, 16, 2), 1: (1, 1, 1), 2: (1, 1, 2), 8: (2, 2, 2), 16: (2, 4, 2)}[n_leaf]
    X, Z, C = dims

    def shards(charges, positions, bases, transfers, couplings, far_source, wanted, near_target, near_slot):
        vmem = pl.BlockSpec(memory_space=pltpu.VMEM)
        hbm = pl.BlockSpec(memory_space=pltpu.HBM)
        rows, points = charges.shape
        dma = pltpu.SemaphoreType.DMA
        return pl.pallas_call(
            functools.partial(kernel, dims),
            out_shape=jax.ShapeDtypeStruct(charges.shape, bf),
            in_specs=[hbm] * 9,
            out_specs=vmem,
            scratch_shapes=[
                pltpu.SMEM(wanted.shape[2:], jnp.int32),
                pltpu.SMEM(far_source.shape, jnp.int32),
                pltpu.VMEM(charges.shape, bf),
                pltpu.VMEM(positions.shape, bf),
                pltpu.VMEM(bases.shape, bf),
                pltpu.VMEM(transfers.shape, bf),
                pltpu.VMEM(near_target.shape[1:], jnp.int32),
                pltpu.VMEM(near_slot.shape[1:], jnp.int32),
                dma((9,)),
            ]
            + [pltpu.VMEM((LEAVES, rows, BS), bf)] * 8
            + [pltpu.VMEM((3 * LEAVES, BS), bf)] * 8
            + [
                pltpu.VMEM((3 * LEAVES, BS), f32),
                pltpu.VMEM((LANES, points), bf),
                pltpu.VMEM((CAP * BS, LANES), bf),
                pltpu.VMEM((rows, CAP * BS), bf),
                pltpu.VMEM((GRP, CAP, points), f32),
                pltpu.VMEM((rows, points), f32),
                pltpu.VMEM((QUARTERS, ROWS, 128), bf),
                pltpu.VMEM((GRP, ROWS, 128), bf),
                pltpu.VMEM((2, ROWS, 128), bf),
                pltpu.VMEM((GRP, 32, 128), bf),
                pltpu.VMEM((X * Z, ROWS, 128), bf),
                pltpu.VMEM((QUARTERS, ROWS, couplings.shape[1]), bf),
                dma((2, 7)),
                dma((2, 7)),
                dma((2, 4)),
                dma((2, 4)),
                dma((GRP,)),
                dma((GRP,)),
                dma((GRP,)),
                dma((GRP,)),
                dma((Z,)),
                dma((Z,)),
                dma((X,)),
                dma((X,)),
                dma,
                dma,
                dma((QUARTERS,)),
                dma((QUARTERS,)),
                pltpu.SemaphoreType.REGULAR,
                pltpu.SemaphoreType.REGULAR,
                pltpu.SemaphoreType.REGULAR,
            ],
            compiler_params=pltpu.CompilerParams(
                collective_id=0, has_side_effects=True, vmem_limit_bytes=56 << 20
            ),
        )(
            wanted[0, 0],
            far_source,
            charges,
            positions,
            bases,
            transfers,
            jnp.swapaxes(couplings[0], 0, 1),
            near_target[0],
            near_slot[0],
        )

    in_specs = (
        P(None, ("leaf", "grp")),
        P(None, ("leaf", "grp")),
        P(None, ("leaf", "grp")),
        P(("leaf", "grp"), None, None),
        P("leaf", "grp", None),
        P("leaf", None),
        P("leaf", "grp", None, None),
        P("leaf", "grp", None),
        P("leaf", "grp", None),
    )
    out_specs = P(None, ("leaf", "grp"))
    return jax.shard_map(shards, mesh=mesh, in_specs=in_specs, out_specs=out_specs, check_vma=False)
```

```python
import functools

import jax
import jax.numpy as jnp
from jax import lax
from jax.experimental import pallas as pl
from jax.experimental.pallas import tpu as pltpu
from jax.sharding import PartitionSpec as P

MESH = pl.DeviceIdType.MESH
bf = jnp.bfloat16
f32 = jnp.float32
GRP = 8
LEAVES = 16
BS = 128
CAP = 8
HALF = LEAVES // 2
FEATS = 9
LANES = 256
QUARTERS = 4
ROWS = 16
SOFTEN2 = 0.05 * 0.05
SCALE = float(BS * BS)
NT = (((1,), (1,)), ((), ()))


def dot_nt(a, b):
    return lax.dot_general(a, b, NT, preferred_element_type=f32)


def dot(a, b):
    return jnp.dot(a, b, preferred_element_type=f32)


def pack(x):
    return jnp.concatenate([x[:32, :], x[32:, :]], axis=1)


def unpack(x):
    return jnp.concatenate([x[:, :64], x[:, 64:]], axis=0)


def pieces(n):
    high = n.astype(bf).astype(f32)
    rest = n - high
    middle = rest.astype(bf).astype(f32)
    return high, middle, rest - middle


def kernel(
    dims,
    wanted_in,
    far_source_in,
    charges_in,
    positions_in,
    bases_in,
    transfers_in,
    couplings_in,
    near_target_in,
    near_slot_in,
    out,
    wanted,
    far_source,
    charges,
    positions,
    bases,
    transfers,
    near_target,
    near_slot,
    in_sem,
    ch0,
    ch1,
    ch2,
    ch3,
    ch4,
    ch5,
    ch6,
    ch7,
    ps0,
    ps1,
    ps2,
    ps3,
    ps4,
    ps5,
    ps6,
    ps7,
    pos_rows,
    target_feat,
    feat_sel,
    charge_sel,
    weight,
    acc,
    up_out,
    part_up,
    sibling,
    part_down,
    coeffs,
    panels,
    ring_send,
    ring_recv,
    pos_send,
    pos_recv,
    up_send,
    up_recv,
    down_send,
    down_recv,
    z_send,
    z_recv,
    x_send,
    x_recv,
    core_send,
    core_recv,
    panel_send,
    panel_recv,
    ready,
):
    X, Z, C = dims
    leaf = lax.axis_index("leaf")
    y = lax.axis_index("grp")
    x = leaf // (Z * C)
    z = (leaf // C) % Z
    core = leaf % C
    quarter = y % QUARTERS
    first_y = y - quarter
    chunk = [ch0, ch1, ch2, ch3, ch4, ch5, ch6, ch7]
    place = [ps0, ps1, ps2, ps3, ps4, ps5, ps6, ps7]

    def y_peer(k):
        return (leaf, (y + k) % GRP)

    def z_peer(k):
        return ((x * Z + (z + k) % Z) * C + core, y)

    def x_peer(k):
        return ((((x + k) % X) * Z + z) * C + core, y)

    core_peer = ((x * Z + z) * C + (1 - core), y)

    ins = [
        (charges_in, charges),
        (positions_in, positions),
        (bases_in, bases),
        (transfers_in, transfers),
        (near_target_in, near_target),
        (near_slot_in, near_slot),
        (wanted_in, wanted),
        (far_source_in, far_source),
        (couplings_in.at[pl.ds(pl.multiple_of(quarter * ROWS, ROWS), ROWS)], panels.at[0]),
    ]

    def fetch(i):
        return pltpu.make_async_copy(ins[i][0], ins[i][1], in_sem.at[i])

    for i in range(len(ins)):
        fetch(i).start()

    barrier = pltpu.get_barrier_semaphore()

    def greet(peer):
        pl.semaphore_signal(barrier, inc=1, device_id=peer, device_id_type=MESH)

    for k in range(1, GRP):
        greet(y_peer(k))
    for k in range(1, X):
        greet(x_peer(k))
    if C > 1:
        greet(core_peer)
    for k in range(1, Z):

        @pl.when(z + k < Z)
        def _():
            greet(z_peer(k))

    for i in range(4):
        fetch(i).wait()

    pos = positions[...].astype(f32)
    for d in range(3):
        for t in range(LEAVES):
            row = d * LEAVES + t
            pos_rows[row : row + 1, :] = pos[d : d + 1, t * BS : (t + 1) * BS]
    ps0[...] = pos_rows[...].astype(bf)
    for t in range(LEAVES):
        ch0[t] = charges[:, t * BS : (t + 1) * BS]

    partial = None
    for t in range(LEAVES):
        cols = slice(t * BS, (t + 1) * BS)
        leaf_coeff = dot_nt(bases[:, cols], charges[:, cols]).astype(bf)
        term = dot(transfers[t], leaf_coeff)
        partial = term if partial is None else partial + term
    partial = jnp.concatenate([partial, partial], axis=1).astype(bf)
    for q in range(QUARTERS):
        up_out[q] = partial[q * ROWS : (q + 1) * ROWS, :]

    pl.semaphore_wait(barrier, (GRP - 1) + (X - 1) + (C - 1) + z)
    for k in range(1, Z):

        @pl.when(k <= z)
        def _():
            pl.semaphore_signal(ready, inc=1, device_id=z_peer(Z - k), device_id_type=MESH)


    def up_copy(k):
        return pltpu.make_async_remote_copy(
            src_ref=up_out.at[(y + k) % QUARTERS],
            dst_ref=part_up.at[k],
            send_sem=up_send.at[k],
            recv_sem=up_recv.at[k],
            device_id=y_peer(k),
            device_id_type=MESH,
        )

    def down_copy(k):
        return pltpu.make_async_remote_copy(
            src_ref=part_down.at[0],
            dst_ref=part_down.at[k],
            send_sem=down_send.at[k],
            recv_sem=down_recv.at[k],
            device_id=y_peer(k),
            device_id_type=MESH,
        )

    def panel_copy(k):
        to = (quarter + k) % QUARTERS
        return pltpu.make_async_remote_copy(
            src_ref=couplings_in.at[pl.ds(pl.multiple_of(to * ROWS, ROWS), ROWS)],
            dst_ref=panels.at[k],
            send_sem=panel_send.at[k],
            recv_sem=panel_recv.at[k],
            device_id=(leaf, first_y + to),
            device_id_type=MESH,
        )

    def ring(right, step, half):
        src = step if right else (GRP - step) % GRP
        dst = step + 1 if right else GRP - step - 1
        part = pl.ds(half * HALF, HALF)
        way = 0 if right else 1
        slot = 2 * step + (half if step < 3 else 0)
        return pltpu.make_async_remote_copy(
            src_ref=chunk[src].at[part],
            dst_ref=chunk[dst].at[part],
            send_sem=ring_send.at[way, slot],
            recv_sem=ring_recv.at[way, slot],
            device_id=y_peer(1 if right else GRP - 1),
            device_id_type=MESH,
        )

    def ring_pos(right, step):
        src = step if right else (GRP - step) % GRP
        dst = step + 1 if right else GRP - step - 1
        way = 0 if right else 1
        return pltpu.make_async_remote_copy(
            src_ref=place[src],
            dst_ref=place[dst],
            send_sem=pos_send.at[way, step],
            recv_sem=pos_recv.at[way, step],
            device_id=y_peer(1 if right else GRP - 1),
            device_id_type=MESH,
        )

    def slot_of(x_at, z_at):
        return x_at * Z + z_at

    def z_copy(up, k, z_at):
        here = coeffs.at[slot_of(x, z_at)]
        return pltpu.make_async_remote_copy(
            src_ref=here,
            dst_ref=here,
            send_sem=z_send.at[up, k],
            recv_sem=z_recv.at[up, k],
            device_id=z_peer(k if up else Z - k),
            device_id_type=MESH,
        )

    def each_z(up, do):
        for k in range(1, Z):

            @pl.when(z + k < Z if up else k <= z)
            def _():
                do(k)

    def x_copy(k, x_at):
        here = coeffs.at[pl.ds(slot_of(x_at, 0), Z)]
        return pltpu.make_async_remote_copy(
            src_ref=here,
            dst_ref=here,
            send_sem=x_send.at[k],
            recv_sem=x_recv.at[k],
            device_id=x_peer(k),
            device_id_type=MESH,
        )

    def core_copy():
        return pltpu.make_async_remote_copy(
            src_ref=sibling.at[0],
            dst_ref=sibling.at[1],
            send_sem=core_send,
            recv_sem=core_recv,
            device_id=core_peer,
            device_id_type=MESH,
        )

    for k in range(1, GRP):
        up_copy(k).start()
    for right in (True, False):
        ring_pos(right, 0).start()
    for half in (0, 1):
        for right in (True, False):
            ring(right, 0, half).start()

    norm = jnp.sum(pos * pos, axis=0, keepdims=True) + SOFTEN2
    high, middle, low = pieces(norm)
    one = jnp.ones_like(norm)
    target_feat[...] = jnp.zeros_like(target_feat)
    for f, v in enumerate((-2.0 * pos[0:1], -2.0 * pos[1:2], -2.0 * pos[2:3], high, middle, low, one, one, one)):
        rows = jnp.broadcast_to(v * SCALE, (LEAVES, v.shape[1]))
        target_feat[f * LEAVES : (f + 1) * LEAVES, :] = rows.astype(bf)

    for i in range(4, 8):
        fetch(i).wait()

    blocks = near_slot.shape[1]
    slot_hot = (
        lax.broadcasted_iota(jnp.int32, (GRP * CAP, blocks), 0) == near_slot[...]
    ).astype(f32)
    leaf_hot = (
        lax.broadcasted_iota(jnp.int32, (LEAVES, blocks), 0) == near_target[...]
    ).astype(f32)
    counts = dot_nt(slot_hot.astype(bf), leaf_hot.astype(bf))
    spread = (
        lax.broadcasted_iota(jnp.int32, (LEAVES, LEAVES * BS), 1) // BS
        == lax.broadcasted_iota(jnp.int32, (LEAVES, LEAVES * BS), 0)
    ).astype(f32)
    spread_counts = dot(counts.astype(bf), spread.astype(bf))
    for h in range(GRP):
        weight[h] = spread_counts[h * CAP : (h + 1) * CAP, :]

    def near(rel, first=False):
        h = (y + (GRP - rel)) % GRP
        rows = place[rel][...].astype(f32)
        px, py, pz = rows[0:16], rows[16:32], rows[32:48]
        ones = jnp.ones_like(px)
        parts = pieces(px * px + py * py + pz * pz)
        pad = jnp.zeros((LANES - FEATS * LEAVES, BS), f32)
        feats = jnp.concatenate((px, py, pz, ones, ones, ones) + parts + (pad,), axis=0)
        feats = feats.T
        lane_leaf = lax.broadcasted_iota(jnp.int32, feats.shape, 1) % LEAVES
        for c in range(CAP):
            at = wanted[h, c]
            charge_sel[:, c * BS : (c + 1) * BS] = chunk[rel][at]
            feat_sel[c * BS : (c + 1) * BS, :] = jnp.where(lane_leaf == at, feats, 0.0).astype(bf)
        width, depth = 2048, 256

        def block(i, carry):
            cols = pl.ds(pl.multiple_of(i * width, width), width)
            targets = target_feat[:, cols]
            w = weight[h, :, cols].astype(bf)
            total = None
            for k in range(0, CAP * BS, depth):
                dist = dot(feat_sel[k : k + depth, :], targets)
                g = lax.rsqrt(dist.astype(bf))
                g = jnp.concatenate(
                    [
                        g[j * BS : (j + 1) * BS, :] * w[k // BS + j : k // BS + j + 1, :]
                        for j in range(depth // BS)
                    ],
                    axis=0,
                )
                term = dot(charge_sel[:, k : k + depth], g)
                total = term if total is None else total + term
            if not first:
                total = total + acc[:, cols]
            acc[:, cols] = total
            return carry

        lax.fori_loop(0, LEAVES * BS // width, block, 0)

    def arrived(step, half, right=True, left=True):
        for way in (True, False):
            if (right if way else left):
                if half == 0 or step == 3:
                    if not (step == 3 and not way):
                        ring_pos(way, step).wait_recv()
                        if step < 2 or (step == 2 and way):
                            ring_pos(way, step + 1).start()
                ring(way, step, half).wait_recv()
                if step < 2:
                    ring(way, step + 1, half).start()
                elif step == 2 and (half == 0) == way:
                    ring(way, 3, half).start()

    near(0, first=True)

    for k in range(1, GRP):
        up_copy(k).wait_recv()
    total = up_out[quarter].astype(f32)
    for k in range(1, GRP):
        total = total + part_up[k].astype(f32)
    if C > 1:
        sibling[0] = total.astype(bf)
        core_copy().start()
    arrived(0, 0)
    if C > 1:
        core_copy().wait_recv()
        side = lax.broadcasted_iota(jnp.int32, total.shape, 1) // (total.shape[1] // 2)
        total = jnp.where(side == core, total.astype(bf).astype(f32), sibling[1].astype(f32))
    coeffs[slot_of(x, z)] = total.astype(bf)
    each_z(0, lambda k: z_copy(0, k, z).start())

    arrived(0, 1)
    for k in range(1, QUARTERS):
        panel_copy(k).start()
    near(1)
    arrived(1, 0)
    near(7)
    arrived(1, 1)
    near(2)
    arrived(2, 0)

    @pl.when(z < Z - 1)
    def _():
        pl.semaphore_wait(ready, Z - 1 - z)

    each_z(1, lambda k: z_copy(1, k, z).start())
    near(6)
    arrived(2, 1)
    each_z(1, lambda k: z_copy(0, k, z + k).wait_recv())
    each_z(0, lambda k: z_copy(1, k, z - k).wait_recv())
    for k in range(1, X):
        x_copy(k, x).start()
    near(3)

    for k in range(1, X):
        x_copy(k, (x + (X - k)) % X).wait_recv()
    fetch(8).wait()
    for k in range(1, QUARTERS):
        panel_copy(k).wait_recv()
    rank = couplings_in.shape[0]
    count = couplings_in.shape[1] // rank
    terms = []
    for odd in (0, 1):
        coeff_rows, panel_rows = [], []
        for k in range(QUARTERS):
            owner = first_y + (quarter + (QUARTERS - k)) % QUARTERS
            for j in range(odd, count, 2):
                source = far_source[0, owner * count + j]
                if C == 1:
                    rows = coeffs[source].astype(f32)[:, :rank]
                else:
                    both = coeffs[source >> 1].astype(f32)
                    rows = jnp.where((source & 1) == 0, both[:, :rank], both[:, rank:])
                coeff_rows.append(rows)
                panel_rows.append(panels[k, :, (j - odd) * rank : (j - odd + 2) * rank])
        left = jnp.concatenate(coeff_rows, axis=0).T.astype(bf)
        terms.append(dot(left, jnp.concatenate(panel_rows, axis=0)))
    part_down[0] = pack(terms[0][:, :rank] + terms[1][:, rank:]).astype(bf)
    for k in range(1, GRP):
        down_copy(k).start()

    near(5)
    arrived(3, 0, left=False)
    arrived(3, 1, right=False)
    near(4)

    for k in range(1, GRP):
        down_copy(k).wait_recv()
    total = part_down[0].astype(f32)
    for k in range(1, GRP):
        total = total + part_down[k].astype(f32)
    target_coeff = unpack(total.astype(bf))
    for t in range(LEAVES):
        cols = slice(t * BS, (t + 1) * BS)
        leaf_target = dot(target_coeff, transfers[t]).astype(bf)
        out[:, cols] = (acc[:, cols] + dot(leaf_target, bases[:, cols])).astype(bf)

    for k in range(1, GRP):
        up_copy(k).wait_send()
        down_copy(k).wait_send()
    for right in (True, False):
        for step in range(3):
            ring_pos(right, step).wait_send()
            for half in (0, 1):
                ring(right, step, half).wait_send()
    ring_pos(True, 3).wait_send()
    ring(True, 3, 0).wait_send()
    ring(False, 3, 1).wait_send()
    for up in (0, 1):
        each_z(up, lambda k: z_copy(up, k, z).wait_send())
    for k in range(1, X):
        x_copy(k, x).wait_send()
    for k in range(1, QUARTERS):
        panel_copy(k).wait_send()
    if C > 1:
        core_copy().wait_send()


def solution(mesh):
    n_leaf = mesh.shape["leaf"]
    dims = {128: (4, 16, 2), 1: (1, 1, 1), 2: (1, 1, 2), 8: (2, 2, 2), 16: (2, 4, 2)}[n_leaf]
    X, Z, C = dims

    def shards(charges, positions, bases, transfers, couplings, far_source, wanted, near_target, near_slot):
        vmem = pl.BlockSpec(memory_space=pltpu.VMEM)
        hbm = pl.BlockSpec(memory_space=pltpu.HBM)
        rows, points = charges.shape
        dma = pltpu.SemaphoreType.DMA
        return pl.pallas_call(
            functools.partial(kernel, dims),
            out_shape=jax.ShapeDtypeStruct(charges.shape, bf),
            in_specs=[hbm] * 9,
            out_specs=vmem,
            scratch_shapes=[
                pltpu.SMEM(wanted.shape[2:], jnp.int32),
                pltpu.SMEM(far_source.shape, jnp.int32),
                pltpu.VMEM(charges.shape, bf),
                pltpu.VMEM(positions.shape, bf),
                pltpu.VMEM(bases.shape, bf),
                pltpu.VMEM(transfers.shape, bf),
                pltpu.VMEM(near_target.shape[1:], jnp.int32),
                pltpu.VMEM(near_slot.shape[1:], jnp.int32),
                dma((9,)),
            ]
            + [pltpu.VMEM((LEAVES, rows, BS), bf)] * 8
            + [pltpu.VMEM((3 * LEAVES, BS), bf)] * 8
            + [
                pltpu.VMEM((3 * LEAVES, BS), f32),
                pltpu.VMEM((LANES, points), bf),
                pltpu.VMEM((CAP * BS, LANES), bf),
                pltpu.VMEM((rows, CAP * BS), bf),
                pltpu.VMEM((GRP, CAP, points), f32),
                pltpu.VMEM((rows, points), f32),
                pltpu.VMEM((QUARTERS, ROWS, 128), bf),
                pltpu.VMEM((GRP, ROWS, 128), bf),
                pltpu.VMEM((2, ROWS, 128), bf),
                pltpu.VMEM((GRP, 32, 128), bf),
                pltpu.VMEM((X * Z, ROWS, 128), bf),
                pltpu.VMEM((QUARTERS, ROWS, couplings.shape[1]), bf),
                dma((2, 7)),
                dma((2, 7)),
                dma((2, 4)),
                dma((2, 4)),
                dma((GRP,)),
                dma((GRP,)),
                dma((GRP,)),
                dma((GRP,)),
                dma((2, Z)),
                dma((2, Z)),
                dma((X,)),
                dma((X,)),
                dma,
                dma,
                dma((QUARTERS,)),
                dma((QUARTERS,)),
                pltpu.SemaphoreType.REGULAR,
            ],
            compiler_params=pltpu.CompilerParams(
                collective_id=0, has_side_effects=True, vmem_limit_bytes=56 << 20
            ),
        )(
            wanted[0, 0],
            far_source,
            charges,
            positions,
            bases,
            transfers,
            jnp.swapaxes(couplings[0], 0, 1),
            near_target[0],
            near_slot[0],
        )

    in_specs = (
        P(None, ("leaf", "grp")),
        P(None, ("leaf", "grp")),
        P(None, ("leaf", "grp")),
        P(("leaf", "grp"), None, None),
        P("leaf", "grp", None),
        P("leaf", None),
        P("leaf", "grp", None, None),
        P("leaf", "grp", None),
        P("leaf", "grp", None),
    )
    out_specs = P(None, ("leaf", "grp"))
    return jax.shard_map(shards, mesh=mesh, in_specs=in_specs, out_specs=out_specs, check_vma=False)
```

```python
import functools

import jax
import jax.numpy as jnp
from jax import lax
from jax.experimental import pallas as pl
from jax.experimental.pallas import tpu as pltpu
from jax.sharding import PartitionSpec as P

MESH = pl.DeviceIdType.MESH
bf = jnp.bfloat16
f32 = jnp.float32
GRP = 8
LEAVES = 16
BS = 128
CAP = 8
HALF = LEAVES // 2
FEATS = 9
LANES = 256
QUARTERS = 4
ROWS = 16
SOFTEN2 = 0.05 * 0.05
SCALE = float(BS * BS)
NT = (((1,), (1,)), ((), ()))


def dot_nt(a, b):
    return lax.dot_general(a, b, NT, preferred_element_type=f32)


def dot(a, b):
    return jnp.dot(a, b, preferred_element_type=f32)


def pack(x):
    return jnp.concatenate([x[:32, :], x[32:, :]], axis=1)


def unpack(x):
    return jnp.concatenate([x[:, :64], x[:, 64:]], axis=0)


def pieces(n):
    high = n.astype(bf).astype(f32)
    rest = n - high
    middle = rest.astype(bf).astype(f32)
    return high, middle, rest - middle


def kernel(
    dims,
    wanted_in,
    far_source_in,
    charges_in,
    positions_in,
    bases_in,
    transfers_in,
    couplings_in,
    near_target_in,
    near_slot_in,
    out,
    wanted,
    far_source,
    charges,
    positions,
    bases,
    transfers,
    near_target,
    near_slot,
    in_sem,
    ch0,
    ch1,
    ch2,
    ch3,
    ch4,
    ch5,
    ch6,
    ch7,
    ps0,
    ps1,
    ps2,
    ps3,
    ps4,
    ps5,
    ps6,
    ps7,
    pos_rows,
    target_feat,
    feat_sel,
    charge_sel,
    weight,
    acc,
    up_out,
    part_up,
    sibling,
    part_down,
    coeffs,
    panels,
    ring_send,
    ring_recv,
    pos_send,
    pos_recv,
    up_send,
    up_recv,
    down_send,
    down_recv,
    z_send,
    z_recv,
    x_send,
    x_recv,
    core_send,
    core_recv,
    panel_send,
    panel_recv,
    ready,
):
    X, Z, C = dims
    leaf = lax.axis_index("leaf")
    y = lax.axis_index("grp")
    x = leaf // (Z * C)
    z = (leaf // C) % Z
    core = leaf % C
    quarter = y % QUARTERS
    first_y = y - quarter
    chunk = [ch0, ch1, ch2, ch3, ch4, ch5, ch6, ch7]
    place = [ps0, ps1, ps2, ps3, ps4, ps5, ps6, ps7]

    def y_peer(k):
        return (leaf, (y + k) % GRP)

    def z_peer(k):
        return ((x * Z + (z + k) % Z) * C + core, y)

    def x_peer(k):
        return ((((x + k) % X) * Z + z) * C + core, y)

    core_peer = ((x * Z + z) * C + (1 - core), y)

    ins = [
        (charges_in, charges),
        (positions_in, positions),
        (bases_in, bases),
        (transfers_in, transfers),
        (near_target_in, near_target),
        (near_slot_in, near_slot),
        (wanted_in, wanted),
        (far_source_in, far_source),
        (couplings_in.at[pl.ds(pl.multiple_of(quarter * ROWS, ROWS), ROWS)], panels.at[0]),
    ]

    def fetch(i):
        return pltpu.make_async_copy(ins[i][0], ins[i][1], in_sem.at[i])

    for i in range(len(ins)):
        fetch(i).start()

    barrier = pltpu.get_barrier_semaphore()

    def greet(peer):
        pl.semaphore_signal(barrier, inc=1, device_id=peer, device_id_type=MESH)

    for k in range(1, GRP):
        greet(y_peer(k))
    for k in range(1, X):
        greet(x_peer(k))
    if C > 1:
        greet(core_peer)
    for k in range(1, Z):

        @pl.when(z + k < Z)
        def _():
            greet(z_peer(k))

    for i in range(4):
        fetch(i).wait()

    pos = positions[...].astype(f32)
    for d in range(3):
        for t in range(LEAVES):
            row = d * LEAVES + t
            pos_rows[row : row + 1, :] = pos[d : d + 1, t * BS : (t + 1) * BS]
    ps0[...] = pos_rows[...].astype(bf)
    for t in range(LEAVES):
        ch0[t] = charges[:, t * BS : (t + 1) * BS]

    partial = None
    for t in range(LEAVES):
        cols = slice(t * BS, (t + 1) * BS)
        leaf_coeff = dot_nt(bases[:, cols], charges[:, cols]).astype(bf)
        term = dot(transfers[t], leaf_coeff)
        partial = term if partial is None else partial + term
    partial = jnp.concatenate([partial, partial], axis=1).astype(bf)
    for q in range(QUARTERS):
        up_out[q] = partial[q * ROWS : (q + 1) * ROWS, :]

    pl.semaphore_wait(barrier, (GRP - 1) + (X - 1) + (C - 1) + z)
    for k in range(1, Z):

        @pl.when(k <= z)
        def _():
            pl.semaphore_signal(ready, inc=1, device_id=z_peer(Z - k), device_id_type=MESH)


    def up_copy(k):
        return pltpu.make_async_remote_copy(
            src_ref=up_out.at[(y + k) % QUARTERS],
            dst_ref=part_up.at[k],
            send_sem=up_send.at[k],
            recv_sem=up_recv.at[k],
            device_id=y_peer(k),
            device_id_type=MESH,
        )

    def down_copy(k):
        return pltpu.make_async_remote_copy(
            src_ref=part_down.at[0],
            dst_ref=part_down.at[k],
            send_sem=down_send.at[k],
            recv_sem=down_recv.at[k],
            device_id=y_peer(k),
            device_id_type=MESH,
        )

    def panel_copy(k):
        to = (quarter + k) % QUARTERS
        return pltpu.make_async_remote_copy(
            src_ref=couplings_in.at[pl.ds(pl.multiple_of(to * ROWS, ROWS), ROWS)],
            dst_ref=panels.at[k],
            send_sem=panel_send.at[k],
            recv_sem=panel_recv.at[k],
            device_id=(leaf, first_y + to),
            device_id_type=MESH,
        )

    def ring(right, step, half):
        src = step if right else (GRP - step) % GRP
        dst = step + 1 if right else GRP - step - 1
        part = pl.ds(half * HALF, HALF)
        way = 0 if right else 1
        slot = 2 * step + (half if step < 3 else 0)
        return pltpu.make_async_remote_copy(
            src_ref=chunk[src].at[part],
            dst_ref=chunk[dst].at[part],
            send_sem=ring_send.at[way, slot],
            recv_sem=ring_recv.at[way, slot],
            device_id=y_peer(1 if right else GRP - 1),
            device_id_type=MESH,
        )

    def ring_pos(right, step):
        src = step if right else (GRP - step) % GRP
        dst = step + 1 if right else GRP - step - 1
        way = 0 if right else 1
        return pltpu.make_async_remote_copy(
            src_ref=place[src],
            dst_ref=place[dst],
            send_sem=pos_send.at[way, step],
            recv_sem=pos_recv.at[way, step],
            device_id=y_peer(1 if right else GRP - 1),
            device_id_type=MESH,
        )

    def slot_of(x_at, z_at):
        return x_at * Z + z_at

    def z_copy(up, k, z_at):
        here = coeffs.at[slot_of(x, z_at)]
        return pltpu.make_async_remote_copy(
            src_ref=here,
            dst_ref=here,
            send_sem=z_send.at[up, k],
            recv_sem=z_recv.at[up, k],
            device_id=z_peer(k if up else Z - k),
            device_id_type=MESH,
        )

    def each_z(up, do):
        for k in range(1, Z):

            @pl.when(z + k < Z if up else k <= z)
            def _():
                do(k)

    def x_copy(k, x_at):
        here = coeffs.at[pl.ds(slot_of(x_at, 0), Z)]
        return pltpu.make_async_remote_copy(
            src_ref=here,
            dst_ref=here,
            send_sem=x_send.at[k],
            recv_sem=x_recv.at[k],
            device_id=x_peer(k),
            device_id_type=MESH,
        )

    def core_copy():
        return pltpu.make_async_remote_copy(
            src_ref=sibling.at[0],
            dst_ref=sibling.at[1],
            send_sem=core_send,
            recv_sem=core_recv,
            device_id=core_peer,
            device_id_type=MESH,
        )

    for k in range(1, GRP):
        up_copy(k).start()
    for right in (True, False):
        ring_pos(right, 0).start()
    for half in (0, 1):
        for right in (True, False):
            ring(right, 0, half).start()

    norm = jnp.sum(pos * pos, axis=0, keepdims=True) + SOFTEN2
    high, middle, low = pieces(norm)
    one = jnp.ones_like(norm)
    target_feat[...] = jnp.zeros_like(target_feat)
    for f, v in enumerate((-2.0 * pos[0:1], -2.0 * pos[1:2], -2.0 * pos[2:3], high, middle, low, one, one, one)):
        rows = jnp.broadcast_to(v * SCALE, (LEAVES, v.shape[1]))
        target_feat[f * LEAVES : (f + 1) * LEAVES, :] = rows.astype(bf)

    for i in range(4, 8):
        fetch(i).wait()

    blocks = near_slot.shape[1]
    slot_hot = (
        lax.broadcasted_iota(jnp.int32, (GRP * CAP, blocks), 0) == near_slot[...]
    ).astype(f32)
    leaf_hot = (
        lax.broadcasted_iota(jnp.int32, (LEAVES, blocks), 0) == near_target[...]
    ).astype(f32)
    counts = dot_nt(slot_hot.astype(bf), leaf_hot.astype(bf))
    spread = (
        lax.broadcasted_iota(jnp.int32, (LEAVES, LEAVES * BS), 1) // BS
        == lax.broadcasted_iota(jnp.int32, (LEAVES, LEAVES * BS), 0)
    ).astype(f32)
    spread_counts = dot(counts.astype(bf), spread.astype(bf))
    for h in range(GRP):
        weight[h] = spread_counts[h * CAP : (h + 1) * CAP, :]

    def near(rel, first=False):
        h = (y + (GRP - rel)) % GRP
        rows = place[rel][...].astype(f32)
        px, py, pz = rows[0:16], rows[16:32], rows[32:48]
        ones = jnp.ones_like(px)
        parts = pieces(px * px + py * py + pz * pz)
        pad = jnp.zeros((LANES - FEATS * LEAVES, BS), f32)
        feats = jnp.concatenate((px, py, pz, ones, ones, ones) + parts + (pad,), axis=0)
        feats = feats.T
        lane_leaf = lax.broadcasted_iota(jnp.int32, feats.shape, 1) % LEAVES
        for c in range(CAP):
            at = wanted[h, c]
            charge_sel[:, c * BS : (c + 1) * BS] = chunk[rel][at]
            feat_sel[c * BS : (c + 1) * BS, :] = jnp.where(lane_leaf == at, feats, 0.0).astype(bf)
        width, depth = 2048, 256

        def block(i, carry):
            cols = pl.ds(pl.multiple_of(i * width, width), width)
            targets = target_feat[:, cols]
            w = weight[h, :, cols].astype(bf)
            total = None
            for k in range(0, CAP * BS, depth):
                dist = dot(feat_sel[k : k + depth, :], targets)
                g = lax.rsqrt(dist.astype(bf))
                g = jnp.concatenate(
                    [
                        g[j * BS : (j + 1) * BS, :] * w[k // BS + j : k // BS + j + 1, :]
                        for j in range(depth // BS)
                    ],
                    axis=0,
                )
                term = dot(charge_sel[:, k : k + depth], g)
                total = term if total is None else total + term
            if not first:
                total = total + acc[:, cols]
            acc[:, cols] = total
            return carry

        lax.fori_loop(0, LEAVES * BS // width, block, 0)

    def arrived(step, half, right=True, left=True):
        for way in (True, False):
            if (right if way else left):
                if half == 0 or step == 3:
                    if not (step == 3 and not way):
                        ring_pos(way, step).wait_recv()
                        if step < 2 or (step == 2 and way):
                            ring_pos(way, step + 1).start()
                ring(way, step, half).wait_recv()
                if step < 2:
                    ring(way, step + 1, half).start()
                elif step == 2 and (half == 0) == way:
                    ring(way, 3, half).start()

    near(0, first=True)
    arrived(0, 0)

    for k in range(1, GRP):
        up_copy(k).wait_recv()
    total = up_out[quarter].astype(f32)
    for k in range(1, GRP):
        total = total + part_up[k].astype(f32)
    if C > 1:
        sibling[0] = total.astype(bf)
        core_copy().start()
    if C > 1:
        core_copy().wait_recv()
        side = lax.broadcasted_iota(jnp.int32, total.shape, 1) // (total.shape[1] // 2)
        total = jnp.where(side == core, total.astype(bf).astype(f32), sibling[1].astype(f32))
    coeffs[slot_of(x, z)] = total.astype(bf)
    each_z(0, lambda k: z_copy(0, k, z).start())

    arrived(0, 1)
    for k in range(1, QUARTERS):
        panel_copy(k).start()
    near(1)
    arrived(1, 0)
    near(7)
    arrived(1, 1)
    near(2)
    arrived(2, 0)

    @pl.when(z < Z - 1)
    def _():
        pl.semaphore_wait(ready, Z - 1 - z)

    each_z(1, lambda k: z_copy(1, k, z).start())
    near(6)
    arrived(2, 1)
    each_z(1, lambda k: z_copy(0, k, z + k).wait_recv())
    each_z(0, lambda k: z_copy(1, k, z - k).wait_recv())
    for k in range(1, X):
        x_copy(k, x).start()
    near(3)

    for k in range(1, X):
        x_copy(k, (x + (X - k)) % X).wait_recv()
    fetch(8).wait()
    for k in range(1, QUARTERS):
        panel_copy(k).wait_recv()
    rank = couplings_in.shape[0]
    count = couplings_in.shape[1] // rank
    terms = []
    for odd in (0, 1):
        coeff_rows, panel_rows = [], []
        for k in range(QUARTERS):
            owner = first_y + (quarter + (QUARTERS - k)) % QUARTERS
            for j in range(odd, count, 2):
                source = far_source[0, owner * count + j]
                if C == 1:
                    rows = coeffs[source].astype(f32)[:, :rank]
                else:
                    both = coeffs[source >> 1].astype(f32)
                    rows = jnp.where((source & 1) == 0, both[:, :rank], both[:, rank:])
                coeff_rows.append(rows)
                panel_rows.append(panels[k, :, (j - odd) * rank : (j - odd + 2) * rank])
        left = jnp.concatenate(coeff_rows, axis=0).T.astype(bf)
        terms.append(dot(left, jnp.concatenate(panel_rows, axis=0)))
    part_down[0] = pack(terms[0][:, :rank] + terms[1][:, rank:]).astype(bf)
    for k in range(1, GRP):
        down_copy(k).start()

    near(5)
    arrived(3, 0, left=False)
    arrived(3, 1, right=False)
    near(4)

    for k in range(1, GRP):
        down_copy(k).wait_recv()
    total = part_down[0].astype(f32)
    for k in range(1, GRP):
        total = total + part_down[k].astype(f32)
    target_coeff = unpack(total.astype(bf))
    for t in range(LEAVES):
        cols = slice(t * BS, (t + 1) * BS)
        leaf_target = dot(target_coeff, transfers[t]).astype(bf)
        out[:, cols] = (acc[:, cols] + dot(leaf_target, bases[:, cols])).astype(bf)

    for k in range(1, GRP):
        up_copy(k).wait_send()
        down_copy(k).wait_send()
    for right in (True, False):
        for step in range(3):
            ring_pos(right, step).wait_send()
            for half in (0, 1):
                ring(right, step, half).wait_send()
    ring_pos(True, 3).wait_send()
    ring(True, 3, 0).wait_send()
    ring(False, 3, 1).wait_send()
    for up in (0, 1):
        each_z(up, lambda k: z_copy(up, k, z).wait_send())
    for k in range(1, X):
        x_copy(k, x).wait_send()
    for k in range(1, QUARTERS):
        panel_copy(k).wait_send()
    if C > 1:
        core_copy().wait_send()


def solution(mesh):
    n_leaf = mesh.shape["leaf"]
    dims = {128: (4, 16, 2), 1: (1, 1, 1), 2: (1, 1, 2), 8: (2, 2, 2), 16: (2, 4, 2)}[n_leaf]
    X, Z, C = dims

    def shards(charges, positions, bases, transfers, couplings, far_source, wanted, near_target, near_slot):
        vmem = pl.BlockSpec(memory_space=pltpu.VMEM)
        hbm = pl.BlockSpec(memory_space=pltpu.HBM)
        rows, points = charges.shape
        dma = pltpu.SemaphoreType.DMA
        return pl.pallas_call(
            functools.partial(kernel, dims),
            out_shape=jax.ShapeDtypeStruct(charges.shape, bf),
            in_specs=[hbm] * 9,
            out_specs=vmem,
            scratch_shapes=[
                pltpu.SMEM(wanted.shape[2:], jnp.int32),
                pltpu.SMEM(far_source.shape, jnp.int32),
                pltpu.VMEM(charges.shape, bf),
                pltpu.VMEM(positions.shape, bf),
                pltpu.VMEM(bases.shape, bf),
                pltpu.VMEM(transfers.shape, bf),
                pltpu.VMEM(near_target.shape[1:], jnp.int32),
                pltpu.VMEM(near_slot.shape[1:], jnp.int32),
                dma((9,)),
            ]
            + [pltpu.VMEM((LEAVES, rows, BS), bf)] * 8
            + [pltpu.VMEM((3 * LEAVES, BS), bf)] * 8
            + [
                pltpu.VMEM((3 * LEAVES, BS), f32),
                pltpu.VMEM((LANES, points), bf),
                pltpu.VMEM((CAP * BS, LANES), bf),
                pltpu.VMEM((rows, CAP * BS), bf),
                pltpu.VMEM((GRP, CAP, points), f32),
                pltpu.VMEM((rows, points), f32),
                pltpu.VMEM((QUARTERS, ROWS, 128), bf),
                pltpu.VMEM((GRP, ROWS, 128), bf),
                pltpu.VMEM((2, ROWS, 128), bf),
                pltpu.VMEM((GRP, 32, 128), bf),
                pltpu.VMEM((X * Z, ROWS, 128), bf),
                pltpu.VMEM((QUARTERS, ROWS, couplings.shape[1]), bf),
                dma((2, 7)),
                dma((2, 7)),
                dma((2, 4)),
                dma((2, 4)),
                dma((GRP,)),
                dma((GRP,)),
                dma((GRP,)),
                dma((GRP,)),
                dma((2, Z)),
                dma((2, Z)),
                dma((X,)),
                dma((X,)),
                dma,
                dma,
                dma((QUARTERS,)),
                dma((QUARTERS,)),
                pltpu.SemaphoreType.REGULAR,
            ],
            compiler_params=pltpu.CompilerParams(
                collective_id=0, has_side_effects=True, vmem_limit_bytes=56 << 20
            ),
        )(
            wanted[0, 0],
            far_source,
            charges,
            positions,
            bases,
            transfers,
            jnp.swapaxes(couplings[0], 0, 1),
            near_target[0],
            near_slot[0],
        )

    in_specs = (
        P(None, ("leaf", "grp")),
        P(None, ("leaf", "grp")),
        P(None, ("leaf", "grp")),
        P(("leaf", "grp"), None, None),
        P("leaf", "grp", None),
        P("leaf", None),
        P("leaf", "grp", None, None),
        P("leaf", "grp", None),
        P("leaf", "grp", None),
    )
    out_specs = P(None, ("leaf", "grp"))
    return jax.shard_map(shards, mesh=mesh, in_specs=in_specs, out_specs=out_specs, check_vma=False)
```
